32 devices in a mesh: lat: 4 (over y, core), lev: 8 (over z, x).
Axes of the slice: x: 2, y: 2, z: 4, core: 2. Of those that a mesh axis runs over, the one named last changes fastest.
Arguments:
- species_fractions: float32 [32, 32, 16, 128], P(None, 'lev', 'lat'), may hold values from 0.1 to 2
- cell_flow_ratios: float32 [2, 32, 16, 128], P(None, 'lev', 'lat'), may hold values from -0.9 to 0.9
- layer_pressure_depth: float32 [32, 16, 128], P(None, 'lat', 'lev'), may hold values from 0.5 to 2
- layer_thickness_fraction: float32 [32], replicated, may hold values from 0.5 to 2
- cell_kelvin_field: float32 [32, 16, 128], P(None, 'lat', 'lev'), may hold values from 200 to 300
- daytime_indicator: int32 [4, 16, 128], P(None, 'lat', 'lev'), may hold values from 0 to 1, as said below
- kinetic_factor_times_step: float32 [256], replicated, may hold values from 0.001 to 0.01
- arrhenius_barrier: float32 [256], replicated, may hold values from 0 to 3
- species_yield_matrix: int32 [256, 32], replicated, may hold values from -2 to 2
- reagent_pairs: int32 [2, 256], replicated, may hold values from 0 to 31
Outputs:
- tracers: float32 [32, 32, 16, 128], P(None, 'lev', 'lat')
The draws below stay inside these ranges and needn't reach their ends.
Inputs may be any that keep to these rules, and one draw needn't show every extreme that they name: `daytime_indicator`: A run of 64 longitudes in a row, cyclic and starting at a drawn longitude (daylight), is active in each substep with probability 7/8 independently; outside it only substep 0 can be active, with probability 1/2.
All inputs are finite; a program needn't handle non-finite values.
Results may differ from the reference program's by a relative error of at most 0.0003.
Values sent between devices are 32-bit elements; how exact they have to be, the bound alone decides.
No kernel may reach another device: no remote copies, remote signals or barrier semaphores. Data moves between devices by JAX's collectives and lax.ppermute only.
A program may use at most 64 MiB of HBM per device.

```python
import math
import jax
import jax.numpy as jnp
from jax import lax

SPEC = 32
LAYER_TOTAL = 32
NREACT = 256
NSUB = 4
PARALLEL_TOTAL = 16
MERIDIAN_TOTAL = 128


def draw_daytime_indicator(key, part):
    offset_key = jax.random.fold_in(key, 11)
    bits_key = jax.random.fold_in(key, 23)
    night_key = jax.random.fold_in(key, 37)
    offset = jax.random.randint(offset_key, (), 0, MERIDIAN_TOTAL)
    longitude = jnp.arange(MERIDIAN_TOTAL, dtype=jnp.int32)
    daylit = (longitude - offset) % MERIDIAN_TOTAL < MERIDIAN_TOTAL // 2
    day_bits = jax.random.randint(bits_key, (NSUB, PARALLEL_TOTAL, MERIDIAN_TOTAL), 0, 8) > 0
    night_bits = jax.random.randint(night_key, (PARALLEL_TOTAL, MERIDIAN_TOTAL), 0, 2) > 0
    first_only = (jnp.arange(NSUB, dtype=jnp.int32) == 0)[:, None, None]
    night_active = night_bits[None] & first_only
    return jnp.where(daylit[None, None, :], day_bits, night_active).astype(jnp.int32)


def place_ends(result, stream_key, smallest, largest):
    longest = result.shape.index(max(result.shape))
    spots = []
    for shift in (0, 1):
        where = [jax.random.randint(jax.random.fold_in(stream_key, axis), (), 0, length) for axis, length in enumerate(result.shape)]
        where[longest] = (where[longest] + shift) % result.shape[longest]
        spots.append(tuple(where))
    return result.at[spots[0]].set(smallest).at[spots[1]].set(largest)


def block_scale(rng, shape, cuts, smallest, largest):
    gain = 1.0
    for position, shards_of in cuts:
        heights = jax.random.uniform(jax.random.fold_in(jax.random.fold_in(rng, 6), position), (shards_of,), jnp.float32, smallest / len(cuts), largest / len(cuts))
        gain = gain * jnp.repeat(jnp.exp(heights), shape[position] // shards_of).reshape((-1,) + (1,) * (len(shape) - 1 - position))
    return gain


def setup_inputs(seed: int = 0) -> dict:
    seeds = jax.random.split(jax.random.key(seed), 11)
    species_fractions = jnp.clip(jnp.exp(math.log(2.0) - 2.9957323 * jax.random.uniform(seeds[0], (SPEC, LAYER_TOTAL, PARALLEL_TOTAL, MERIDIAN_TOTAL), jnp.float32) ** block_scale(seeds[0], (SPEC, LAYER_TOTAL, PARALLEL_TOTAL, MERIDIAN_TOTAL), ((1, 8), (2, 4)), -0.2, 0.2)), 0.1, 2.0)
    cell_flow_ratios = jnp.clip(jax.random.uniform(seeds[1], (2, LAYER_TOTAL, PARALLEL_TOTAL, MERIDIAN_TOTAL), jnp.float32, -0.9, 0.9) * block_scale(seeds[1], (2, LAYER_TOTAL, PARALLEL_TOTAL, MERIDIAN_TOTAL), ((1, 8), (2, 4)), -0.4, 0.0), -0.9, 0.9)
    layer_pressure_depth = jnp.clip(jnp.exp(math.log(2.0) - 1.3862944 * jax.random.uniform(seeds[2], (LAYER_TOTAL, PARALLEL_TOTAL, MERIDIAN_TOTAL), jnp.float32) ** block_scale(seeds[2], (LAYER_TOTAL, PARALLEL_TOTAL, MERIDIAN_TOTAL), ((1, 4), (2, 8)), -0.2, 0.2)), 0.5, 2.0)
    layer_thickness_fraction = jnp.clip(jnp.exp(jax.random.uniform(seeds[3], (LAYER_TOTAL,), jnp.float32, math.log(0.5), math.log(2.0))), 0.5, 2.0)
    cell_kelvin_field = jnp.clip(200.0 + 100.0 * jax.random.uniform(seeds[4], (LAYER_TOTAL, PARALLEL_TOTAL, MERIDIAN_TOTAL), jnp.float32) ** block_scale(seeds[4], (LAYER_TOTAL, PARALLEL_TOTAL, MERIDIAN_TOTAL), ((1, 4), (2, 8)), -0.2, 0.2), 200.0, 300.0)
    daytime_indicator = draw_daytime_indicator(jax.random.fold_in(seeds[10], 71), 0)
    kinetic_factor_times_step = jnp.clip(jnp.exp(jax.random.uniform(seeds[6], (NREACT,), jnp.float32, math.log(0.001), math.log(0.01))), 0.001, 0.01)
    arrhenius_barrier = jnp.clip(jax.random.uniform(seeds[7], (NREACT,), jnp.float32, 0.0, 3.0), 0.0, 3.0)
    species_yield_matrix = place_ends(jax.random.randint(seeds[8], (NREACT, SPEC), -2, 3), jax.random.fold_in(seeds[8], 1), -2, 2).astype(jnp.int32)
    reagent_pairs = place_ends(jax.random.randint(seeds[9], (2, NREACT), 0, SPEC), jax.random.fold_in(seeds[9], 1), 0, SPEC - 1).astype(jnp.int32)
    return dict(species_fractions=species_fractions, cell_flow_ratios=cell_flow_ratios, layer_pressure_depth=layer_pressure_depth, layer_thickness_fraction=layer_thickness_fraction, cell_kelvin_field=cell_kelvin_field, daytime_indicator=daytime_indicator, kinetic_factor_times_step=kinetic_factor_times_step, arrhenius_barrier=arrhenius_barrier, species_yield_matrix=species_yield_matrix, reagent_pairs=reagent_pairs)


def minmod(left, right):
    return 0.5 * (jnp.sign(left) + jnp.sign(right)) * jnp.minimum(jnp.abs(left), jnp.abs(right))


def face_flux(courant, before, before_slope, after_cell, after_slope):
    forward = courant * (before + 0.5 * (1.0 - courant) * before_slope)
    backward = courant * (after_cell - 0.5 * (1.0 + courant) * after_slope)
    return jnp.where(courant > 0.0, forward, backward)


def lon_update(tracer, zonal_wind):
    before = jnp.roll(tracer, 1, axis=-1)
    behind = jnp.roll(tracer, -1, axis=-1)
    slopes = minmod(tracer - before, behind - tracer)
    courant = 0.5 * (jnp.roll(zonal_wind, 1, axis=-1) + zonal_wind)
    fluxes = face_flux(courant, before, jnp.roll(slopes, 1, axis=-1), tracer, slopes)
    return tracer - (jnp.roll(fluxes, -1, axis=-1) - fluxes)


def lat_update(padded, merid_wind, face_ok):
    row_count = padded.shape[-2]
    slopes = minmod(padded[..., 1:-1, :] - padded[..., :-2, :], padded[..., 2:, :] - padded[..., 1:-1, :])
    courant = 0.5 * (merid_wind[..., 1:row_count - 2, :] + merid_wind[..., 2:row_count - 1, :]) * face_ok[2:row_count - 1][:, None]
    fluxes = face_flux(courant, padded[..., 1:row_count - 2, :], slopes[..., 0:row_count - 3, :], padded[..., 2:row_count - 1, :], slopes[..., 1:row_count - 2, :])
    return padded[..., 2:row_count - 2, :] - (fluxes[..., 1:, :] - fluxes[..., :-1, :])


def advect_species(tracer, cell_flow_ratios, face_ok):
    for sweep_index in range(2):
        tracer = lon_update(tracer, cell_flow_ratios[0])
        padded = jnp.pad(tracer, ((0, 0), (2, 2), (0, 0)))
        merid_wind = jnp.pad(cell_flow_ratios[1], ((0, 0), (2, 2), (0, 0)))
        tracer = lat_update(padded, merid_wind, face_ok)
    return tracer


def remap(vertical_profiles, layer_pressure_depth, layer_thickness_fraction):
    upper_edge = jnp.cumsum(layer_pressure_depth, axis=0)
    lower_edge = jnp.concatenate([jnp.zeros_like(upper_edge[:1]), upper_edge[:-1]], axis=0)
    column_total = upper_edge[-1]
    expand = (slice(None),) + (None,) * column_total.ndim
    share_sum = jnp.sum(layer_thickness_fraction)
    fraction_top = jnp.cumsum(layer_thickness_fraction) / share_sum
    fraction_bottom = jnp.concatenate([jnp.zeros((1,), fraction_top.dtype), fraction_top[:-1]])
    target_top = fraction_top[expand] * column_total[None]
    target_bottom = fraction_bottom[expand] * column_total[None]
    intersection = jnp.maximum(0.0, jnp.minimum(upper_edge[None], target_top[:, None]) - jnp.maximum(lower_edge[None], target_bottom[:, None]))
    target_thick = (layer_thickness_fraction / share_sum)[expand] * column_total[None]
    carried = jnp.einsum("ts...,ns...->nt...", intersection, vertical_profiles, precision=lax.Precision.HIGHEST)
    return carried / target_thick[None]


def perform_kinetics(vertical_profiles, cell_kelvin_field, daytime_indicator, kinetic_factor_times_step, arrhenius_barrier, yield_matrix_floating, first_axis_position, final_axis_position):
    species = vertical_profiles.shape[0]
    flattened = vertical_profiles.reshape(species, -1)
    reciprocal_specific_warmth = (300.0 / cell_kelvin_field).reshape(1, -1) - 1.0
    constants = kinetic_factor_times_step[:, None] * jnp.exp(-arrhenius_barrier[:, None] * reciprocal_specific_warmth)
    for kinetics_minor_step in range(daytime_indicator.shape[0]):
        switched_on = jnp.broadcast_to(daytime_indicator[kinetics_minor_step][None], cell_kelvin_field.shape).reshape(1, -1) > 0
        rates = constants * jnp.take(flattened, first_axis_position, axis=0) * jnp.take(flattened, final_axis_position, axis=0)
        change = jnp.dot(yield_matrix_floating.T, rates, precision=lax.Precision.HIGHEST)
        flattened = jnp.where(switched_on, flattened + change, flattened)
    return flattened.reshape(vertical_profiles.shape)


def reference(species_fractions, cell_flow_ratios, layer_pressure_depth, layer_thickness_fraction, cell_kelvin_field, daytime_indicator, kinetic_factor_times_step, arrhenius_barrier, species_yield_matrix, reagent_pairs):
    global_row = jnp.arange(PARALLEL_TOTAL + 4, dtype=jnp.int32) - 2
    face_ok = ((global_row >= 1) & (global_row <= PARALLEL_TOTAL - 1)).astype(species_fractions.dtype)
    carried_species_field = lax.map(lambda tracer: advect_species(tracer, cell_flow_ratios, face_ok), species_fractions)
    yield_matrix_floating = species_yield_matrix.astype(species_fractions.dtype)

    def along_parallels(row_items):
        vertical_profiles, thick_row, temp_row, mask_row = row_items
        remapped = remap(vertical_profiles, thick_row, layer_thickness_fraction)
        return perform_kinetics(remapped, temp_row, mask_row, kinetic_factor_times_step, arrhenius_barrier, yield_matrix_floating, reagent_pairs[0], reagent_pairs[1])

    result_sequence = lax.map(along_parallels, (jnp.moveaxis(carried_species_field, 2, 0), jnp.moveaxis(layer_pressure_depth, 1, 0), jnp.moveaxis(cell_kelvin_field, 1, 0), jnp.moveaxis(daytime_indicator, 1, 0)))
    return jnp.moveaxis(result_sequence, 0, 2)
```

```python
import jax
import jax.numpy as jnp
from jax import lax
from jax.sharding import PartitionSpec as P


def padded_2(value, sides, width):
    for axis, dim in sides:
        size, length = (lax.axis_size(axis), value.shape[dim])
        up = [(i, (i + 1) % size) for i in range(size - 1)]
        down = [(j, i) for i, j in up]
        last = lax.slice_in_dim(value, length - width, length, axis=dim)
        first = lax.slice_in_dim(value, 0, width, axis=dim)
        before = lax.ppermute(last, axis, up)
        after = lax.ppermute(first, axis, down)
        value = jnp.concatenate([before, value, after], axis=dim)
    return value


def minmod(left, right):
    return 0.5 * (jnp.sign(left) + jnp.sign(right)) * jnp.minimum(jnp.abs(left), jnp.abs(right))


def face_flux(courant, before, before_slope, after_cell, after_slope):
    forward = courant * (before + 0.5 * (1.0 - courant) * before_slope)
    backward = courant * (after_cell - 0.5 * (1.0 + courant) * after_slope)
    return jnp.where(courant > 0.0, forward, backward)


def lon_update(tracer, zonal_wind):
    before = jnp.roll(tracer, 1, axis=-1)
    behind = jnp.roll(tracer, -1, axis=-1)
    slopes = minmod(tracer - before, behind - tracer)
    courant = 0.5 * (jnp.roll(zonal_wind, 1, axis=-1) + zonal_wind)
    fluxes = face_flux(courant, before, jnp.roll(slopes, 1, axis=-1), tracer, slopes)
    return tracer - (jnp.roll(fluxes, -1, axis=-1) - fluxes)


def lat_update(padded, merid_wind, face_ok):
    row_count = padded.shape[-2]
    slopes = minmod(
        padded[..., 1:-1, :] - padded[..., :-2, :], padded[..., 2:, :] - padded[..., 1:-1, :]
    )
    courant = (
        0.5
        * (merid_wind[..., 1 : row_count - 2, :] + merid_wind[..., 2 : row_count - 1, :])
        * face_ok[2 : row_count - 1][:, None]
    )
    fluxes = face_flux(
        courant,
        padded[..., 1 : row_count - 2, :],
        slopes[..., 0 : row_count - 3, :],
        padded[..., 2 : row_count - 1, :],
        slopes[..., 1 : row_count - 2, :],
    )
    return padded[..., 2 : row_count - 2, :] - (fluxes[..., 1:, :] - fluxes[..., :-1, :])


def running_sum(value):
    rows = [value[0]]
    for item in range(1, value.shape[0]):
        rows.append(rows[-1] + value[item])
    return jnp.stack(rows)


def remap(vertical_profiles, layer_pressure_depth, layer_thickness_fraction):
    upper_edge = running_sum(layer_pressure_depth)
    lower_edge = jnp.concatenate([jnp.zeros_like(upper_edge[:1]), upper_edge[:-1]], axis=0)
    column_total = upper_edge[-1]
    expand = (slice(None),) + (None,) * column_total.ndim
    share_sum = jnp.sum(layer_thickness_fraction)
    fraction_top = running_sum(layer_thickness_fraction) / share_sum
    fraction_bottom = jnp.concatenate([jnp.zeros((1,), fraction_top.dtype), fraction_top[:-1]])
    target_top = fraction_top[expand] * column_total[None]
    target_bottom = fraction_bottom[expand] * column_total[None]
    intersection = jnp.maximum(
        0.0,
        jnp.minimum(upper_edge[None], target_top[:, None])
        - jnp.maximum(lower_edge[None], target_bottom[:, None]),
    )
    target_thick = (layer_thickness_fraction / share_sum)[expand] * column_total[None]
    carried = jnp.einsum(
        "ts...,ns...->nt...", intersection, vertical_profiles, precision=lax.Precision.HIGHEST
    )
    return carried / target_thick[None]


def react_block(
    vertical_profiles,
    cell_kelvin_field,
    daytime_indicator,
    kinetic_factor_times_step,
    arrhenius_barrier,
    yield_matrix_floating,
    first_axis_position,
    final_axis_position,
):
    species = vertical_profiles.shape[0]
    flattened = vertical_profiles.reshape(species, -1)
    reciprocal_specific_warmth = (300.0 / cell_kelvin_field).reshape(1, -1) - 1.0
    constants = kinetic_factor_times_step[:, None] * jnp.exp(
        -arrhenius_barrier[:, None] * reciprocal_specific_warmth
    )
    for kinetics_minor_step in range(daytime_indicator.shape[0]):
        switched_on = (
            jnp.broadcast_to(
                daytime_indicator[kinetics_minor_step][None], cell_kelvin_field.shape
            ).reshape(1, -1)
            > 0.5
        )

        rates = (
            constants
            * jnp.take(flattened, first_axis_position, axis=0)
            * jnp.take(flattened, final_axis_position, axis=0)
        )
        change = jnp.dot(yield_matrix_floating.T, rates, precision=lax.Precision.HIGHEST)
        flattened = jnp.where(switched_on, flattened + change, flattened)
    return flattened.reshape(vertical_profiles.shape)


def back_to_levels(vertical_profiles):
    return lax.all_to_all(vertical_profiles, "lev", split_axis=1, concat_axis=3, tiled=True)


def body(
    species_fractions,
    cell_flow_ratios,
    layer_pressure_depth,
    layer_thickness_fraction,
    cell_kelvin_field,
    daytime_indicator,
    kinetic_factor_times_step,
    arrhenius_barrier,
    species_yield_matrix,
    reagent_pairs,
):
    band_rows = species_fractions.shape[2]
    lat_start = lax.axis_index("lat") * band_rows
    lat_total = band_rows * lax.axis_size("lat")
    tracer = species_fractions
    merid_wind = padded_2(cell_flow_ratios[1], (("lat", 1),), 1)
    merid_wind = jnp.pad(merid_wind, ((0, 0), (1, 1), (0, 0)))
    global_row = lat_start + jnp.arange(band_rows + 4, dtype=jnp.int32) - 2
    rim_mask = ((global_row >= 1) & (global_row <= lat_total - 1)).astype(jnp.float32)
    for sweep_index in range(2):
        tracer = lon_update(tracer, cell_flow_ratios[0])
        padded = padded_2(tracer, (("lat", 2),), 2)
        tracer = lat_update(padded, merid_wind, rim_mask)
    vertical_profiles = lax.all_to_all(tracer, "lev", split_axis=3, concat_axis=1, tiled=True)
    vertical_profiles = remap(vertical_profiles, layer_pressure_depth, layer_thickness_fraction)
    yield_matrix_floating = species_yield_matrix.astype(jnp.float32)
    first_axis_position = reagent_pairs[0]
    final_axis_position = reagent_pairs[1]
    mask_float = daytime_indicator.astype(jnp.float32)
    vertical_profiles = react_block(
        vertical_profiles,
        cell_kelvin_field,
        mask_float,
        kinetic_factor_times_step,
        arrhenius_barrier,
        yield_matrix_floating,
        first_axis_position,
        final_axis_position,
    )
    return back_to_levels(vertical_profiles)


def solution(mesh):
    placed = (
        P(None, "lev", "lat", None),
        P(None, "lev", "lat", None),
        P(None, "lat", "lev"),
        P(),
        P(None, "lat", "lev"),
        P(None, "lat", "lev"),
        P(),
        P(),
        P(),
        P(),
    )
    return jax.shard_map(
        body, mesh=mesh, in_specs=placed, out_specs=P(None, "lev", "lat", None), check_vma=False
    )
```

```python
import functools

import jax
import jax.numpy as jnp
from jax import lax
from jax.experimental import pallas as pl
from jax.experimental.pallas import tpu as pltpu
from jax.sharding import PartitionSpec as P

LANES = 128
OCTET = 8
SWEEPS = 2
VMEM = pl.BlockSpec(memory_space=pltpu.VMEM)


def limited_slope(left, right):
    return jnp.maximum(jnp.minimum(left, right), 0.0) + jnp.minimum(jnp.maximum(left, right), 0.0)


def upwind_weights(courant):
    ahead = jnp.maximum(courant, 0.0)
    behind = jnp.minimum(courant, 0.0)
    return ahead, 0.5 * ahead * (1.0 - courant), behind, -0.5 * behind * (1.0 + courant)


def block_transpose(tiles, width):
    tiles = list(tiles)
    lane_block = lax.broadcasted_iota(jnp.int32, tiles[0].shape, 1) // width
    step = 1
    while step < len(tiles):
        upper = (lane_block // step) % 2 == 1
        for low in range(len(tiles)):
            if low & step:
                continue
            first, second = tiles[low], tiles[low + step]
            tiles[low] = jnp.where(upper, pltpu.roll(second, step * width, 1), first)
            tiles[low + step] = jnp.where(
                upper, second, pltpu.roll(first, LANES - step * width, 1)
            )
        step *= 2
    return tiles


def lon_step(f, weights):
    ahead, ahead_slope, behind, behind_slope = weights
    size = f.shape[1]
    left = f - pltpu.roll(f, 1, 1)
    slope = limited_slope(left, pltpu.roll(left, size - 1, 1))
    east = ahead * f + ahead_slope * slope
    west = behind * f + behind_slope * slope
    return f - ((east - pltpu.roll(east, 1, 1)) + (pltpu.roll(west, size - 1, 1) - west))


def lat_step(f, first_row, weights_at):
    jumps = [f[i + 1] - f[i] for i in range(len(f) - 1)]
    slopes = [None] + [limited_slope(jumps[i - 1], jumps[i]) for i in range(1, len(f) - 1)]
    fluxes = []
    for i in range(2, len(f) - 1):
        ahead, ahead_slope, behind, behind_slope = weights_at(first_row + i)
        fluxes.append(
            (ahead * f[i - 1] + ahead_slope * slopes[i - 1])
            + (behind * f[i] + behind_slope * slopes[i])
        )
    return [f[i] - (fluxes[i - 1] - fluxes[i - 2]) for i in range(2, len(f) - 2)]


def advect_kernel(
    sizes, own_ref, core_ref, chip_ref, own_wind, core_wind, chip_wind, out_ref, wind, zonal, merid
):
    species, levels, rows, parts, width = sizes
    halo = 2 * SWEEPS
    band = lax.axis_index("lat")
    even = band % 2 == 0
    plane = levels * rows

    per_band = 2 * plane * parts
    wind[0:per_band] = jnp.where(even, chip_wind[...], core_wind[...])
    wind[per_band : 2 * per_band] = own_wind[...]
    wind[2 * per_band : 3 * per_band] = jnp.where(even, core_wind[...], chip_wind[...])

    for source in range(3):
        flow = jnp.concatenate(
            [wind[pl.ds(source * per_band + k, plane, parts), :] for k in range(parts)], axis=1
        )
        size = flow.shape[1]
        west_face = 0.5 * (pltpu.roll(flow, 1, 1) + flow)
        east_face = pltpu.roll(west_face, size - 1, 1)
        there = slice(source * plane, (source + 1) * plane)
        zonal[0, there], zonal[1, there] = upwind_weights(east_face)[:2]
        zonal[2, there], zonal[3, there] = upwind_weights(west_face)[2:]

    def flow_row(row):
        source, inside = divmod(row + rows, rows)
        start = source * per_band + (plane + inside) * parts
        return jnp.concatenate(
            [wind[pl.ds(start + k, levels, rows * parts), :] for k in range(parts)], axis=1
        )

    total = rows * lax.axis_size("lat")
    low_face = 2 - halo
    for face in range(low_face, rows + halo - 1):
        place = band * rows + face
        open_face = jnp.logical_and(place >= 1, place <= total - 1).astype(jnp.float32)
        courant = 0.5 * (flow_row(face - 1) + flow_row(face)) * open_face
        for which, weight in enumerate(upwind_weights(courant)):
            merid[which, face - low_face] = weight

    def octet_rows(ref, octet, level, row):
        start = (octet * OCTET * plane + level * rows + row) * parts
        return jnp.concatenate(
            [ref[pl.ds(start + k, OCTET, plane * parts), :] for k in range(parts)], axis=1
        )

    def step(index, carry):
        pair, octet = index // (species // OCTET), index % (species // OCTET)
        done = []
        for parity in range(2):
            level = pair * 2 + parity

            def zonal_at(row):
                source, inside = divmod(row + rows, rows)
                at = source * plane + level * rows + inside
                return [zonal[which, pl.ds(at, 1), :] for which in range(4)]

            def merid_at(face):
                return [merid[which, face - low_face, pl.ds(level, 1), :] for which in range(4)]

            before, after = [], []
            for row in range(rows):
                by_core = octet_rows(core_ref, octet, level, row)
                by_chip = octet_rows(chip_ref, octet, level, row)
                before.append(jnp.where(even, by_chip, by_core))
                after.append(jnp.where(even, by_core, by_chip))
            here = [octet_rows(own_ref, octet, level, row) for row in range(rows)]
            f = before[rows - halo :] + here + after[:halo]
            first_row = -halo
            for sweep in range(SWEEPS):
                f = [lon_step(item, zonal_at(first_row + i)) for i, item in enumerate(f)]
                f = lat_step(f, first_row, merid_at)
                first_row += 2
            done += f
        start = pl.multiple_of(pair * species + octet * OCTET, OCTET)
        per_part = LANES // width
        for k in range(parts):
            cut = [item[:, k * LANES : (k + 1) * LANES] for item in done]
            for j, tile in enumerate(block_transpose(cut, width)):
                out_ref[k * per_part + j, pl.ds(start, OCTET), :] = tile
        return carry

    lax.fori_loop(0, (levels // 2) * (species // OCTET), step, 0)


def spread_kernel(sizes, in_ref, out_ref):
    species, levels, rows, parts, width = sizes
    plane = levels * rows
    per_part = LANES // width
    for pair in range(levels // 2):
        for octet in range(species // OCTET):
            for k in range(parts):
                start = pair * species + octet * OCTET
                cut = [in_ref[k * per_part + j, start : start + OCTET, :] for j in range(per_part)]
                for g, tile in enumerate(block_transpose(cut, width)):
                    at = (octet * OCTET * plane + pair * 2 * rows + g) * parts + k
                    out_ref[pl.ds(at, OCTET, plane * parts), :] = tile


def column_kernel(
    sizes,
    moved_ref,
    depth_ref,
    share_ref,
    kelvin_ref,
    active_ref,
    factor_ref,
    barrier_ref,
    pick_ref,
    yield_ref,
    out_ref,
    lower_ref,
    overlap_ref,
    rate_ref,
):
    pairs, species, tile_pairs = sizes
    half = LANES // 2
    levels = 2 * pairs
    reactions = factor_ref.shape[0]
    odd = lax.broadcasted_iota(jnp.int32, (1, LANES), 1) >= half

    depth = depth_ref[...]
    other = pltpu.roll(depth, half, 1)
    both = depth + other
    edge = jnp.zeros((1, LANES), jnp.float32)
    for s in range(pairs):
        lower_ref[s : s + 1] = edge
        edge = edge + both[s : s + 1]
    total = edge
    lower = lower_ref[...] + jnp.where(odd, other, 0.0)
    upper = lower + depth

    share_sum = share_ref[0:1]
    for t in range(1, levels):
        share_sum = share_sum + share_ref[t : t + 1]
    below = jnp.zeros((1, LANES), jnp.float32)
    target_low = below
    for t in range(levels):
        share = share_ref[t : t + 1]
        below = below + share
        target_top = below / share_sum * total
        shared = jnp.maximum(
            jnp.minimum(upper, target_top) - jnp.maximum(lower, target_low), 0.0
        )
        overlap_ref[t] = shared / (share / share_sum * total)
        target_low = target_top

    def tile_step(tile, carry):
        held = []
        for inside in range(tile_pairs):
            t = tile * tile_pairs + inside
            sums = []
            for parity in range(2):
                acc = None
                for s in range(pairs):
                    term = overlap_ref[2 * t + parity, s : s + 1, :] * moved_ref[s]
                    acc = term if acc is None else acc + term
                sums.append(acc)
            kept = jnp.where(odd, sums[1], sums[0])
            crossed = jnp.where(odd, sums[0], sums[1])
            held.append(kept + pltpu.roll(crossed, half, 1))

        for inside in range(tile_pairs):
            t = tile * tile_pairs + inside
            warmth = 300.0 / kelvin_ref[pl.ds(t, 1), :] - 1.0
            rate_ref[:, inside * LANES : (inside + 1) * LANES] = factor_ref[...] * jnp.exp(
                -barrier_ref[...] * warmth
            )
        q = jnp.concatenate(held, axis=1)
        for substep in range(active_ref.shape[0]):
            on = jnp.concatenate([active_ref[substep : substep + 1, :]] * tile_pairs, axis=1)
            high = q.astype(jnp.bfloat16)
            low = (q - high.astype(jnp.float32)).astype(jnp.bfloat16)
            picked = jnp.dot(
                pick_ref[...],
                jnp.concatenate([high, low], axis=0),
                preferred_element_type=jnp.float32,
            )
            rates = rate_ref[...] * picked[:reactions] * picked[reactions:]
            high = rates.astype(jnp.bfloat16)
            low = (rates - high.astype(jnp.float32)).astype(jnp.bfloat16)
            change = jnp.dot(
                yield_ref[...],
                jnp.concatenate([high, low], axis=0),
                preferred_element_type=jnp.float32,
            )
            q = jnp.where(on > 0, q + change, q)
        for inside in range(tile_pairs):
            out_ref[tile * tile_pairs + inside] = q[:, inside * LANES : (inside + 1) * LANES]
        return carry

    lax.fori_loop(0, pairs // tile_pairs, tile_step, 0)


def swap_pairs(count, first):
    route = []
    for low in range(first, count - 1, 2):
        route += [(low, low + 1), (low + 1, low)]
    return route


def body(
    species_fractions,
    cell_flow_ratios,
    layer_pressure_depth,
    layer_thickness_fraction,
    cell_kelvin_field,
    daytime_indicator,
    kinetic_factor_times_step,
    arrhenius_barrier,
    species_yield_matrix,
    reagent_pairs,
):
    species, levels, rows, lons = species_fractions.shape
    all_levels = layer_pressure_depth.shape[0]
    width = layer_pressure_depth.shape[2]
    blocks = lax.axis_size("lev")
    bands = lax.axis_size("lat")
    parts = lons // LANES
    substeps = daytime_indicator.shape[0]
    reactions = kinetic_factor_times_step.shape[0]
    assert 2 * rows * width == LANES and levels % 2 == 0 and rows == 2 * SWEEPS
    sizes = (species, levels, rows, parts, width)

    by_core, by_chip = swap_pairs(bands, 0), swap_pairs(bands, 1)
    core_wind = lax.ppermute(cell_flow_ratios, "lat", by_core)
    chip_wind = lax.ppermute(cell_flow_ratios, "lat", by_chip)
    core_band = lax.ppermute(species_fractions, "lat", by_core)
    chip_band = lax.ppermute(species_fractions, "lat", by_chip)

    def flat(value):
        return value.reshape(-1, LANES)

    packed = pl.pallas_call(
        functools.partial(advect_kernel, sizes),
        out_shape=jax.ShapeDtypeStruct((blocks, levels // 2 * species, LANES), jnp.float32),
        in_specs=[VMEM] * 6,
        out_specs=VMEM,
        scratch_shapes=[
            pltpu.VMEM((3 * 2 * levels * rows * parts, LANES), jnp.float32),
            pltpu.VMEM((4, 3 * levels * rows, lons), jnp.float32),
            pltpu.VMEM((4, 3 * rows - 3, levels, lons), jnp.float32),
        ],
        name="advect",
    )(
        flat(species_fractions),
        flat(core_band),
        flat(chip_band),
        flat(cell_flow_ratios),
        flat(core_wind),
        flat(chip_wind),
    )
    moved = lax.all_to_all(packed, "lev", split_axis=0, concat_axis=0, tiled=True)

    pairs = all_levels // 2
    first_pick = reagent_pairs.reshape(-1)[:, None] == (
        lax.broadcasted_iota(jnp.int32, (2 * reactions, 2 * species), 1) % species
    )
    yields = species_yield_matrix.T.astype(jnp.bfloat16)
    active = daytime_indicator.reshape(substeps, -1)
    tile_pairs = 4
    reacted = pl.pallas_call(
        functools.partial(column_kernel, (pairs, species, tile_pairs)),
        out_shape=jax.ShapeDtypeStruct((pairs, species, LANES), jnp.float32),
        in_specs=[VMEM] * 9,
        out_specs=VMEM,
        scratch_shapes=[
            pltpu.VMEM((pairs, LANES), jnp.float32),
            pltpu.VMEM((all_levels, pairs, LANES), jnp.float32),
            pltpu.VMEM((reactions, tile_pairs * LANES), jnp.float32),
        ],
        compiler_params=pltpu.CompilerParams(vmem_limit_bytes=32 * 2**20),
        name="columns",
    )(
        moved.reshape(pairs, species, LANES),
        layer_pressure_depth.reshape(pairs, LANES),
        jnp.broadcast_to(layer_thickness_fraction[:, None], (all_levels, LANES)),
        cell_kelvin_field.reshape(pairs, LANES),
        jnp.concatenate([active, active], axis=1),
        jnp.broadcast_to(kinetic_factor_times_step[:, None], (reactions, LANES)),
        jnp.broadcast_to(arrhenius_barrier[:, None], (reactions, LANES)),
        first_pick.astype(jnp.bfloat16),
        jnp.concatenate([yields, yields], axis=1),
    )
    returned = lax.all_to_all(
        reacted.reshape(packed.shape), "lev", split_axis=0, concat_axis=0, tiled=True
    )
    out = pl.pallas_call(
        functools.partial(spread_kernel, sizes),
        out_shape=jax.ShapeDtypeStruct((species * levels * rows * parts, LANES), jnp.float32),
        in_specs=[VMEM],
        out_specs=VMEM,
        name="spread",
    )(returned)
    return out.reshape(species_fractions.shape)


def solution(mesh):
    placed = (
        P(None, "lev", "lat", None),
        P(None, "lev", "lat", None),
        P(None, "lat", "lev"),
        P(),
        P(None, "lat", "lev"),
        P(None, "lat", "lev"),
        P(),
        P(),
        P(),
        P(),
    )
    return jax.shard_map(
        body, mesh=mesh, in_specs=placed, out_specs=P(None, "lev", "lat", None), check_vma=False
    )
```

```python
import functools

import jax
import jax.numpy as jnp
from jax import lax
from jax.experimental import pallas as pl
from jax.experimental.pallas import tpu as pltpu
from jax.sharding import PartitionSpec as P

LANES = 128
OCTET = 8
SWEEPS = 2
VMEM = pl.BlockSpec(memory_space=pltpu.VMEM)
PARAMS = pltpu.CompilerParams(vmem_limit_bytes=16 * 2**20)


def limited_slope(left, right):
    return jnp.maximum(jnp.minimum(left, right), 0.0) + jnp.minimum(jnp.maximum(left, right), 0.0)


def upwind_weights(courant):
    ahead = jnp.maximum(courant, 0.0)
    behind = jnp.minimum(courant, 0.0)
    return ahead, 0.5 * ahead * (1.0 - courant), behind, -0.5 * behind * (1.0 + courant)


def block_transpose(tiles, width):
    tiles = list(tiles)
    lane_block = lax.broadcasted_iota(jnp.int32, tiles[0].shape, 1) // width
    step = 1
    while step < len(tiles):
        upper = (lane_block // step) % 2 == 1
        for low in range(len(tiles)):
            if low & step:
                continue
            first, second = tiles[low], tiles[low + step]
            tiles[low] = jnp.where(upper, pltpu.roll(second, step * width, 1), first)
            tiles[low + step] = jnp.where(
                upper, second, pltpu.roll(first, LANES - step * width, 1)
            )
        step *= 2
    return tiles


def lon_step(f, weights):
    ahead, ahead_slope, behind, behind_slope = weights
    size = f.shape[1]
    left = f - pltpu.roll(f, 1, 1)
    slope = limited_slope(left, pltpu.roll(left, size - 1, 1))
    east = ahead * f + ahead_slope * slope
    west = behind * f + behind_slope * slope
    return f - ((east - pltpu.roll(east, 1, 1)) + (pltpu.roll(west, size - 1, 1) - west))


def lat_step(f, first_row, weights_at):
    jumps = [f[i + 1] - f[i] for i in range(len(f) - 1)]
    slopes = [None] + [limited_slope(jumps[i - 1], jumps[i]) for i in range(1, len(f) - 1)]
    fluxes = []
    for i in range(2, len(f) - 1):
        ahead, ahead_slope, behind, behind_slope = weights_at(first_row + i)
        fluxes.append(
            (ahead * f[i - 1] + ahead_slope * slopes[i - 1])
            + (behind * f[i] + behind_slope * slopes[i])
        )
    return [f[i] - (fluxes[i - 1] - fluxes[i - 2]) for i in range(2, len(f) - 2)]


def advect_kernel(
    sizes, own_ref, core_ref, chip_ref, own_wind, core_wind, chip_wind, out_ref, wind, zonal, merid
):
    species, levels, rows, parts, width = sizes
    halo = 2 * SWEEPS
    band = lax.axis_index("lat")
    even = band % 2 == 0
    plane = levels * rows

    per_band = 2 * plane * parts
    wind[0:per_band] = jnp.where(even, chip_wind[...], core_wind[...])
    wind[per_band : 2 * per_band] = own_wind[...]
    wind[2 * per_band : 3 * per_band] = jnp.where(even, core_wind[...], chip_wind[...])

    for source in range(3):
        flow = jnp.concatenate(
            [wind[pl.ds(source * per_band + k, plane, parts), :] for k in range(parts)], axis=1
        )
        size = flow.shape[1]
        west_face = 0.5 * (pltpu.roll(flow, 1, 1) + flow)
        east_face = pltpu.roll(west_face, size - 1, 1)
        there = slice(source * plane, (source + 1) * plane)
        zonal[0, there], zonal[1, there] = upwind_weights(east_face)[:2]
        zonal[2, there], zonal[3, there] = upwind_weights(west_face)[2:]

    def flow_row(row):
        source, inside = divmod(row + rows, rows)
        start = source * per_band + (plane + inside) * parts
        return jnp.concatenate(
            [wind[pl.ds(start + k, levels, rows * parts), :] for k in range(parts)], axis=1
        )

    total = rows * lax.axis_size("lat")
    low_face = 2 - halo
    for face in range(low_face, rows + halo - 1):
        place = band * rows + face
        open_face = jnp.logical_and(place >= 1, place <= total - 1).astype(jnp.float32)
        courant = 0.5 * (flow_row(face - 1) + flow_row(face)) * open_face
        for which, weight in enumerate(upwind_weights(courant)):
            merid[which, face - low_face] = weight

    def octet_rows(ref, octet, level, row):
        start = (octet * OCTET * plane + level * rows + row) * parts
        return jnp.concatenate(
            [ref[pl.ds(start + k, OCTET, plane * parts), :] for k in range(parts)], axis=1
        )

    def step(index, carry):
        pair, octet = index // (species // OCTET), index % (species // OCTET)
        done = []
        for parity in range(2):
            level = pair * 2 + parity

            def zonal_at(row):
                source, inside = divmod(row + rows, rows)
                at = source * plane + level * rows + inside
                return [zonal[which, pl.ds(at, 1), :] for which in range(4)]

            def merid_at(face):
                return [merid[which, face - low_face, pl.ds(level, 1), :] for which in range(4)]

            before, after = [], []
            for row in range(rows):
                by_core = octet_rows(core_ref, octet, level, row)
                by_chip = octet_rows(chip_ref, octet, level, row)
                before.append(jnp.where(even, by_chip, by_core))
                after.append(jnp.where(even, by_core, by_chip))
            here = [octet_rows(own_ref, octet, level, row) for row in range(rows)]
            f = before[rows - halo :] + here + after[:halo]
            first_row = -halo
            for sweep in range(SWEEPS):
                f = [lon_step(item, zonal_at(first_row + i)) for i, item in enumerate(f)]
                f = lat_step(f, first_row, merid_at)
                first_row += 2
            done += f
        start = pl.multiple_of(pair * species + octet * OCTET, OCTET)
        per_part = LANES // width
        for k in range(parts):
            cut = [item[:, k * LANES : (k + 1) * LANES] for item in done]
            for j, tile in enumerate(block_transpose(cut, width)):
                out_ref[k * per_part + j, pl.ds(start, OCTET), :] = tile
        return carry

    lax.fori_loop(0, (levels // 2) * (species // OCTET), step, 0)


def spread_kernel(sizes, in_ref, out_ref):
    species, levels, rows, parts, width = sizes
    plane = levels * rows
    per_part = LANES // width
    for pair in range(levels // 2):
        for octet in range(species // OCTET):
            for k in range(parts):
                start = pair * species + octet * OCTET
                cut = [in_ref[k * per_part + j, start : start + OCTET, :] for j in range(per_part)]
                for g, tile in enumerate(block_transpose(cut, width)):
                    at = (octet * OCTET * plane + pair * 2 * rows + g) * parts + k
                    out_ref[pl.ds(at, OCTET, plane * parts), :] = tile


def column_kernel(
    sizes,
    moved_ref,
    depth_ref,
    share_ref,
    kelvin_ref,
    active_ref,
    factor_ref,
    barrier_ref,
    pick_ref,
    yield_ref,
    out_ref,
    lower_ref,
    overlap_ref,
    rate_ref,
):
    pairs, species, tile_pairs = sizes
    half = LANES // 2
    levels = 2 * pairs
    reactions = factor_ref.shape[0]
    odd = lax.broadcasted_iota(jnp.int32, (1, LANES), 1) >= half

    depth = depth_ref[...]
    other = pltpu.roll(depth, half, 1)
    both = depth + other
    edge = jnp.zeros((1, LANES), jnp.float32)
    for s in range(pairs):
        lower_ref[s : s + 1] = edge
        edge = edge + both[s : s + 1]
    total = edge
    lower = lower_ref[...] + jnp.where(odd, other, 0.0)
    upper = lower + depth

    share_sum = share_ref[0:1]
    for t in range(1, levels):
        share_sum = share_sum + share_ref[t : t + 1]
    below = jnp.zeros((1, LANES), jnp.float32)
    target_low = below
    for t in range(levels):
        share = share_ref[t : t + 1]
        below = below + share
        target_top = below / share_sum * total
        shared = jnp.maximum(
            jnp.minimum(upper, target_top) - jnp.maximum(lower, target_low), 0.0
        )
        overlap_ref[t] = shared / (share / share_sum * total)
        target_low = target_top

    def tile_step(tile, carry):
        held = []
        for inside in range(tile_pairs):
            t = tile * tile_pairs + inside
            sums = []
            for parity in range(2):
                acc = None
                for s in range(pairs):
                    term = overlap_ref[2 * t + parity, s : s + 1, :] * moved_ref[s]
                    acc = term if acc is None else acc + term
                sums.append(acc)
            kept = jnp.where(odd, sums[1], sums[0])
            crossed = jnp.where(odd, sums[0], sums[1])
            held.append(kept + pltpu.roll(crossed, half, 1))

        for inside in range(tile_pairs):
            t = tile * tile_pairs + inside
            warmth = 300.0 / kelvin_ref[pl.ds(t, 1), :] - 1.0
            rate_ref[:, inside * LANES : (inside + 1) * LANES] = factor_ref[...] * jnp.exp(
                -barrier_ref[...] * warmth
            )
        q = jnp.concatenate(held, axis=1)
        for substep in range(active_ref.shape[0]):
            on = jnp.concatenate([active_ref[substep : substep + 1, :]] * tile_pairs, axis=1)
            high = q.astype(jnp.bfloat16)
            low = (q - high.astype(jnp.float32)).astype(jnp.bfloat16)
            picked = jnp.dot(
                pick_ref[...],
                jnp.concatenate([high, low], axis=0),
                preferred_element_type=jnp.float32,
            )
            rates = rate_ref[...] * picked[:reactions] * picked[reactions:]
            high = rates.astype(jnp.bfloat16)
            low = (rates - high.astype(jnp.float32)).astype(jnp.bfloat16)
            change = jnp.dot(
                yield_ref[...],
                jnp.concatenate([high, low], axis=0),
                preferred_element_type=jnp.float32,
            )
            q = jnp.where(on > 0, q + change, q)
        for inside in range(tile_pairs):
            out_ref[tile * tile_pairs + inside] = q[:, inside * LANES : (inside + 1) * LANES]
        return carry

    lax.fori_loop(0, pairs // tile_pairs, tile_step, 0)


def swap_pairs(count, first):
    route = []
    for low in range(first, count - 1, 2):
        route += [(low, low + 1), (low + 1, low)]
    return route


def body(
    species_fractions,
    cell_flow_ratios,
    layer_pressure_depth,
    layer_thickness_fraction,
    cell_kelvin_field,
    daytime_indicator,
    kinetic_factor_times_step,
    arrhenius_barrier,
    species_yield_matrix,
    reagent_pairs,
):
    species, levels, rows, lons = species_fractions.shape
    all_levels = layer_pressure_depth.shape[0]
    width = layer_pressure_depth.shape[2]
    blocks = lax.axis_size("lev")
    bands = lax.axis_size("lat")
    parts = lons // LANES
    substeps = daytime_indicator.shape[0]
    reactions = kinetic_factor_times_step.shape[0]
    assert 2 * rows * width == LANES and levels % 2 == 0 and rows == 2 * SWEEPS
    sizes = (species, levels, rows, parts, width)

    by_core, by_chip = swap_pairs(bands, 0), swap_pairs(bands, 1)
    core_wind = lax.ppermute(cell_flow_ratios, "lat", by_core)
    chip_wind = lax.ppermute(cell_flow_ratios, "lat", by_chip)
    core_band = lax.ppermute(species_fractions, "lat", by_core)
    chip_band = lax.ppermute(species_fractions, "lat", by_chip)

    def flat(value):
        return value.reshape(-1, LANES)

    packed = pl.pallas_call(
        functools.partial(advect_kernel, sizes),
        out_shape=jax.ShapeDtypeStruct((blocks, levels // 2 * species, LANES), jnp.float32),
        in_specs=[VMEM] * 6,
        out_specs=VMEM,
        scratch_shapes=[
            pltpu.VMEM((3 * 2 * levels * rows * parts, LANES), jnp.float32),
            pltpu.VMEM((4, 3 * levels * rows, lons), jnp.float32),
            pltpu.VMEM((4, 3 * rows - 3, levels, lons), jnp.float32),
        ],
        compiler_params=PARAMS,
        name="advect",
    )(
        flat(species_fractions),
        flat(core_band),
        flat(chip_band),
        flat(cell_flow_ratios),
        flat(core_wind),
        flat(chip_wind),
    )
    moved = lax.all_to_all(packed, "lev", split_axis=0, concat_axis=0, tiled=True)

    pairs = all_levels // 2
    first_pick = reagent_pairs.reshape(-1)[:, None] == (
        lax.broadcasted_iota(jnp.int32, (2 * reactions, 2 * species), 1) % species
    )
    yields = species_yield_matrix.T.astype(jnp.bfloat16)
    active = daytime_indicator.reshape(substeps, -1)
    tile_pairs = pairs // 2
    reacted = pl.pallas_call(
        functools.partial(column_kernel, (pairs, species, tile_pairs)),
        out_shape=jax.ShapeDtypeStruct((pairs, species, LANES), jnp.float32),
        in_specs=[VMEM] * 9,
        out_specs=VMEM,
        scratch_shapes=[
            pltpu.VMEM((pairs, LANES), jnp.float32),
            pltpu.VMEM((all_levels, pairs, LANES), jnp.float32),
            pltpu.VMEM((reactions, tile_pairs * LANES), jnp.float32),
        ],
        compiler_params=PARAMS,
        name="columns",
    )(
        moved.reshape(pairs, species, LANES),
        layer_pressure_depth.reshape(pairs, LANES),
        jnp.broadcast_to(layer_thickness_fraction[:, None], (all_levels, LANES)),
        cell_kelvin_field.reshape(pairs, LANES),
        jnp.concatenate([active, active], axis=1),
        jnp.broadcast_to(kinetic_factor_times_step[:, None], (reactions, LANES)),
        jnp.broadcast_to(arrhenius_barrier[:, None], (reactions, LANES)),
        first_pick.astype(jnp.bfloat16),
        jnp.concatenate([yields, yields], axis=1),
    )
    returned = lax.all_to_all(
        reacted.reshape(packed.shape), "lev", split_axis=0, concat_axis=0, tiled=True
    )
    out = pl.pallas_call(
        functools.partial(spread_kernel, sizes),
        out_shape=jax.ShapeDtypeStruct((species * levels * rows * parts, LANES), jnp.float32),
        in_specs=[VMEM],
        out_specs=VMEM,
        compiler_params=PARAMS,
        name="spread",
    )(returned)
    return out.reshape(species_fractions.shape)


def solution(mesh):
    placed = (
        P(None, "lev", "lat", None),
        P(None, "lev", "lat", None),
        P(None, "lat", "lev"),
        P(),
        P(None, "lat", "lev"),
        P(None, "lat", "lev"),
        P(),
        P(),
        P(),
        P(),
    )
    return jax.shard_map(
        body, mesh=mesh, in_specs=placed, out_specs=P(None, "lev", "lat", None), check_vma=False
    )
```

```python
import functools

import jax
import jax.numpy as jnp
from jax import lax
from jax.experimental import pallas as pl
from jax.experimental.pallas import tpu as pltpu
from jax.sharding import PartitionSpec as P

LANES = 128
PAD = 8
SWEEPS = 2
PARAMS = pltpu.CompilerParams(vmem_limit_bytes=16 * 2**20)
F32 = jnp.float32


def limited_slope(left, right):
    return jnp.maximum(jnp.minimum(left, right), 0.0) + jnp.minimum(jnp.maximum(left, right), 0.0)


def slope_weight(courant):
    return courant * (0.5 * (jnp.where(courant > 0.0, 1.0, -1.0) - courant))


def face_flux(courant, weight, before, after, before_slope, after_slope):
    ahead = courant > 0.0
    return courant * jnp.where(ahead, before, after) + weight * jnp.where(
        ahead, before_slope, after_slope
    )


def put_cyclic(ref, row, value):
    size = value.shape[0]
    ref[row, PAD : PAD + size] = value
    ref[row, PAD - 1 : PAD] = value[size - 1 :]
    ref[row, PAD + size : PAD + size + 1] = value[:1]


def shifted(ref, row, size, by):
    return ref[row, PAD + by : PAD + by + size]


def lon_step(f_ref, slope_ref, flux_ref, row, courant, weight):
    size = courant.shape[0]
    f, left, right = (shifted(f_ref, row, size, by) for by in (0, -1, 1))
    slope = limited_slope(f - left, right - f)
    put_cyclic(slope_ref, row, slope)
    flux = face_flux(courant, weight, left, f, shifted(slope_ref, row, size, -1), slope)
    put_cyclic(flux_ref, row, flux)
    return f - (shifted(flux_ref, row, size, 1) - flux)


def lat_step(f, weights):
    jumps = [f[i + 1] - f[i] for i in range(len(f) - 1)]
    slopes = [None] + [limited_slope(jumps[i - 1], jumps[i]) for i in range(1, len(f) - 1)]
    fluxes = [
        face_flux(*weights[i - 2], f[i - 1], f[i], slopes[i - 1], slopes[i])
        for i in range(2, len(f) - 1)
    ]
    return [f[i] - (fluxes[i - 1] - fluxes[i - 2]) for i in range(2, len(f) - 2)]


def tracer_rows(sizes, ref, row):
    species, levels, rows, parts, _ = sizes
    return [
        ref[pl.ds(row * parts + k, species * levels, rows * parts), :] for k in range(parts)
    ]


def flow_rows(sizes, ref, which, row):
    species, levels, rows, parts, _ = sizes
    found = []
    for k in range(parts):
        start = (which * levels * rows + row) * parts + k
        level_rows = ref[pl.ds(start, levels, rows * parts), :]
        tile = jnp.concatenate([level_rows] * (8 // levels), axis=0)
        found.append(jnp.concatenate([tile] * (species * levels // 8), axis=0))
    return found


def turned(tiles):
    return jnp.concatenate([tile.T for tile in tiles], axis=0)


def zonal_weights(flow_ref, row, flow):
    put_cyclic(flow_ref, row, flow)
    courant = 0.5 * (shifted(flow_ref, row, flow.shape[0], -1) + flow)
    return courant, slope_weight(courant)


def own_kernel(
    sizes, band_ref, wind_ref, f_out, zonal_out, merid_out, f_ref, slope_ref, flux_ref, flow_ref
):
    rows = sizes[2]
    for row in range(rows):
        courant, weight = zonal_weights(
            flow_ref, row, turned(flow_rows(sizes, wind_ref, 0, row))
        )
        zonal_out[row, 0], zonal_out[row, 1] = courant, weight
        merid_out[row] = turned(flow_rows(sizes, wind_ref, 1, row))
        put_cyclic(f_ref, row, turned(tracer_rows(sizes, band_ref, row)))
        f_out[row] = lon_step(f_ref, slope_ref, flux_ref, row, courant, weight)


def advect_kernel(
    sizes,
    own_ref,
    own_zonal,
    own_merid,
    core_ref,
    chip_ref,
    core_wind,
    chip_wind,
    out_ref,
    f_ref,
    slope_ref,
    flux_ref,
    flow_ref,
    halo_zonal,
    halo_merid,
    merid_ref,
    next_ref,
):
    species, levels, rows, parts, width = sizes
    band = lax.axis_index("lat")
    even = band % 2 == 0

    def both_sides(by_core, by_chip):
        pairs = list(zip(by_core, by_chip, strict=True))
        before = [jnp.where(even, chip, core) for core, chip in pairs]
        after = [jnp.where(even, core, chip) for core, chip in pairs]
        return before, after

    for row in range(rows):
        zonal = both_sides(
            flow_rows(sizes, core_wind, 0, row), flow_rows(sizes, chip_wind, 0, row)
        )
        merid = both_sides(
            flow_rows(sizes, core_wind, 1, row), flow_rows(sizes, chip_wind, 1, row)
        )
        tracer = both_sides(
            tracer_rows(sizes, core_ref, row), tracer_rows(sizes, chip_ref, row)
        )
        for side in range(2):
            at = side * rows + row
            courant, weight = zonal_weights(flow_ref, at, turned(zonal[side]))
            halo_zonal[at, 0], halo_zonal[at, 1] = courant, weight
            halo_merid[at] = turned(merid[side])
            put_cyclic(f_ref, at, turned(tracer[side]))
            f_ref[at, PAD : PAD + courant.shape[0]] = lon_step(
                f_ref, slope_ref, flux_ref, at, courant, weight
            )

    def row_of(halo, own, row):
        if 0 <= row < rows:
            return own, row
        return halo, (row + rows if row < 0 else row)

    total = rows * lax.axis_size("lat")
    size = own_ref.shape[1]
    first_face, last_face = 2 - 2 * SWEEPS, rows + 2 * SWEEPS - 2
    for chunk in range(size // width):
        there = slice(chunk * width, (chunk + 1) * width)
        inner = slice(PAD + chunk * width, PAD + (chunk + 1) * width)

        def merid_at(row):
            ref, at = row_of(halo_merid, own_merid, row)
            return ref[at, there]

        weights = []
        for face in range(first_face, last_face + 1):
            place = band * rows + face
            open_face = jnp.logical_and(place >= 1, place <= total - 1).astype(F32)
            courant = 0.5 * (merid_at(face - 1) + merid_at(face)) * open_face
            weights.append((courant, slope_weight(courant)))
            if 0 <= face <= rows:
                merid_ref[face, 0, there], merid_ref[face, 1, there] = weights[-1]
        f = []
        for row in range(-rows, 2 * rows):
            ref, at = row_of(f_ref, own_ref, row)
            f.append(ref[at, there if ref is own_ref else inner])
        for at, value in enumerate(lat_step(f, weights)):
            next_ref[at, inner] = value

    swept = rows + 2 * SWEEPS
    for at in range(swept):
        next_ref[at, PAD - 1 : PAD] = next_ref[at, PAD + size - 1 : PAD + size]
        next_ref[at, PAD + size : PAD + size + 1] = next_ref[at, PAD : PAD + 1]
        ref, there = row_of(halo_zonal, own_zonal, at - 2)
        f_ref[at, PAD : PAD + size] = lon_step(
            next_ref, slope_ref, flux_ref, at, ref[there, 0], ref[there, 1]
        )
    for chunk in range(size // width):
        there = slice(chunk * width, (chunk + 1) * width)
        inner = slice(PAD + chunk * width, PAD + (chunk + 1) * width)
        f = [f_ref[at, inner] for at in range(swept)]
        weights = [
            (merid_ref[face, 0, there], merid_ref[face, 1, there]) for face in range(rows + 1)
        ]
        for row, value in enumerate(lat_step(f, weights)):
            out_ref[chunk, row * width : (row + 1) * width] = value


def spread_kernel(sizes, in_ref, out_ref):
    species, levels, rows, parts, width = sizes
    per_part = LANES // width
    for row in range(rows):
        for k in range(parts):
            found = [
                in_ref[k * per_part + j, row * width : (row + 1) * width] for j in range(per_part)
            ]
            out_ref[pl.ds(row * parts + k, species * levels, rows * parts), :] = jnp.concatenate(
                found, axis=0
            ).T


def paired(groups, levels, ref, place):
    rows, width = ref.shape[1], ref.shape[2]
    for pair in range(groups // 2):
        for parity in range(2):
            start = (2 * pair + parity) * levels
            for row in range(rows):
                lane = (parity * rows + row) * width
                place[pair * levels : (pair + 1) * levels, lane : lane + width] = ref[
                    start : start + levels, row, :
                ]


def prepare_kernel(
    groups,
    depth_ref,
    share_ref,
    kelvin_ref,
    active_ref,
    factor_ref,
    barrier_ref,
    yield_ref,
    pair_ref,
    overlap_out,
    rate_out,
    active_out,
    pick_out,
    yield_out,
    depth_at,
    kelvin_at,
    lower_at,
):
    all_levels, rows, width = depth_ref.shape
    levels = all_levels // groups
    half = LANES // 2
    odd = lax.broadcasted_iota(jnp.int32, (1, LANES), 1) >= half
    reactions, species = yield_ref.shape

    paired(groups, levels, kelvin_ref, kelvin_at)
    paired(groups, levels, depth_ref, depth_at)
    for parity in range(2):
        for row in range(rows):
            lane = (parity * rows + row) * width
            active_out[:, lane : lane + width] = active_ref[:, row, :]

    def column(ref):
        return jnp.broadcast_to(ref[...], (LANES, ref.shape[1])).T

    base = jnp.zeros((1, LANES), F32)
    for pair in range(groups // 2):
        inside = jnp.zeros((1, LANES), F32)
        for level in range(levels):
            at = pair * levels + level
            lower_at[at : at + 1] = inside
            inside = inside + depth_at[at : at + 1]
        other = pltpu.roll(inside, half, 1)
        start = base + jnp.where(odd, other, 0.0)
        here = slice(pair * levels, (pair + 1) * levels)
        lower_at[here] = lower_at[here] + start
        base = base + (inside + other)
    total = base
    lower = lower_at[...]
    upper = lower + depth_at[...]

    share = column(share_ref)
    share_sum = share[0:1]
    for t in range(1, all_levels):
        share_sum = share_sum + share[t : t + 1]
    below = jnp.zeros((1, LANES), F32)
    target_low = below
    for t in range(all_levels):
        below = below + share[t : t + 1]
        target_top = below / share_sum * total
        shared = jnp.maximum(
            jnp.minimum(upper, target_top) - jnp.maximum(lower, target_low), 0.0
        )
        overlap_out[t] = shared / (share[t : t + 1] / share_sum * total)
        target_low = target_top

    factor, barrier = column(factor_ref), column(barrier_ref)
    for at in range(kelvin_at.shape[0]):
        warmth = 300.0 / kelvin_at[at : at + 1] - 1.0
        rate_out[:, at * LANES : (at + 1) * LANES] = factor * jnp.exp(-barrier * warmth)

    one_species = lax.broadcasted_iota(jnp.int32, (2 * species, reactions), 0) % species
    for which in range(2):
        hit = (one_species == pair_ref[which : which + 1, :]).astype(F32)
        pick_out[which * reactions : (which + 1) * reactions] = hit.T.astype(jnp.bfloat16)
    yields = yield_ref[...].astype(F32).T.astype(jnp.bfloat16)
    yield_out[:, :reactions] = yields
    yield_out[:, reactions:] = yields


def column_kernel(
    sizes,
    moved_ref,
    overlap_ref,
    rate_ref,
    active_ref,
    pick_ref,
    yield_ref,
    out_ref,
    source_ref,
    target_ref,
):
    groups, levels, species, tile_pairs = sizes
    half = LANES // 2
    pairs = groups // 2 * levels
    reactions = yield_ref.shape[1] // 2
    odd = lax.broadcasted_iota(jnp.int32, (1, LANES), 1) >= half

    for pair in range(groups // 2):
        both = jnp.concatenate([moved_ref[2 * pair], moved_ref[2 * pair + 1]], axis=0)
        source_ref[pair] = both.T

    def remapped(at):
        pair, level = divmod(at, levels)
        sums = []
        for parity in range(2):
            t = (2 * pair + parity) * levels + level
            acc = None
            for s in range(pairs):
                source = source_ref[s // levels, pl.ds(s % levels, species, levels), :]
                term = overlap_ref[t, s : s + 1, :] * source
                acc = term if acc is None else acc + term
            sums.append(acc)
        kept = jnp.where(odd, sums[1], sums[0])
        crossed = jnp.where(odd, sums[0], sums[1])
        return kept + pltpu.roll(crossed, half, 1)

    for first in range(0, pairs, tile_pairs):
        tile = range(first, first + tile_pairs)
        lanes = slice(first * LANES, (first + tile_pairs) * LANES)
        q = jnp.concatenate([remapped(at) for at in tile], axis=1)
        for substep in range(active_ref.shape[0]):
            on = jnp.concatenate([active_ref[substep : substep + 1, :]] * tile_pairs, axis=1)
            high = q.astype(jnp.bfloat16)
            low = (q - high.astype(F32)).astype(jnp.bfloat16)
            picked = jnp.dot(
                pick_ref[...], jnp.concatenate([high, low], axis=0), preferred_element_type=F32
            )
            rates = rate_ref[:, lanes] * picked[:reactions] * picked[reactions:]
            high = rates.astype(jnp.bfloat16)
            low = (rates - high.astype(F32)).astype(jnp.bfloat16)
            change = jnp.dot(
                yield_ref[...], jnp.concatenate([high, low], axis=0), preferred_element_type=F32
            )
            q = jnp.where(on > 0, q + change, q)
        for at in tile:
            pair, level = divmod(at, levels)
            lane = (at - first) * LANES
            target_ref[pair, pl.ds(level, species, levels), :] = q[:, lane : lane + LANES]

    for pair in range(groups // 2):
        both = target_ref[pair].T
        out_ref[2 * pair], out_ref[2 * pair + 1] = both[:half], both[half:]


def swap_pairs(count, first):
    route = []
    for low in range(first, count - 1, 2):
        route += [(low, low + 1), (low + 1, low)]
    return route


def kernel_call(kernel, name, outs, scratch, cost=None):
    return pl.pallas_call(
        kernel,
        out_shape=outs,
        scratch_shapes=[pltpu.VMEM(shape, F32) for shape in scratch],
        compiler_params=PARAMS,
        cost_estimate=cost,
        name=name,
    )


def body(
    species_fractions,
    cell_flow_ratios,
    layer_pressure_depth,
    layer_thickness_fraction,
    cell_kelvin_field,
    daytime_indicator,
    kinetic_factor_times_step,
    arrhenius_barrier,
    species_yield_matrix,
    reagent_pairs,
):
    species, levels, rows, lons = species_fractions.shape
    all_levels = layer_pressure_depth.shape[0]
    width = layer_pressure_depth.shape[2]
    blocks = lax.axis_size("lev")
    bands = lax.axis_size("lat")
    parts = lons // LANES
    substeps = daytime_indicator.shape[0]
    reactions = kinetic_factor_times_step.shape[0]
    assert 2 * rows * width == LANES and rows == 2 * SWEEPS and blocks % 2 == 0
    sizes = (species, levels, rows, parts, width)
    mixed = species * levels

    by_core, by_chip = swap_pairs(bands, 0), swap_pairs(bands, 1)
    core_band = lax.ppermute(species_fractions, "lat", by_core)
    chip_band = lax.ppermute(species_fractions, "lat", by_chip)
    core_wind = lax.ppermute(cell_flow_ratios, "lat", by_core)
    chip_wind = lax.ppermute(cell_flow_ratios, "lat", by_chip)

    def flat(value):
        return value.reshape(-1, LANES)

    def arrays(*shapes):
        return [jax.ShapeDtypeStruct(shape, F32) for shape in shapes]

    padded = lons + 2 * PAD
    own = kernel_call(
        functools.partial(own_kernel, sizes),
        "own_rows",
        arrays((rows, lons, mixed), (rows, 2, lons, mixed), (rows, lons, mixed)),
        [(rows, padded, mixed)] * 4,
        pl.CostEstimate(flops=10**7, bytes_accessed=2 * 10**6, transcendentals=0),
    )(flat(species_fractions), flat(cell_flow_ratios))

    packed = kernel_call(
        functools.partial(advect_kernel, sizes),
        "advect",
        arrays((blocks, rows * width, mixed))[0],
        [(2 * rows, padded, mixed)] * 4
        + [
            (2 * rows, 2, lons, mixed),
            (2 * rows, lons, mixed),
            (rows + 1, 2, lons, mixed),
            (2 * rows, padded, mixed),
        ],
    )(*own, flat(core_band), flat(chip_band), flat(core_wind), flat(chip_wind))
    moved = lax.all_to_all(packed, "lev", split_axis=0, concat_axis=0, tiled=True)

    pairs = all_levels // 2
    prepared = kernel_call(
        functools.partial(prepare_kernel, blocks),
        "prepare",
        [
            *arrays((all_levels, pairs, LANES), (reactions, pairs * LANES)),
            jax.ShapeDtypeStruct((substeps, LANES), jnp.int32),
            jax.ShapeDtypeStruct((2 * reactions, 2 * species), jnp.bfloat16),
            jax.ShapeDtypeStruct((species, 2 * reactions), jnp.bfloat16),
        ],
        [(pairs, LANES)] * 3,
        pl.CostEstimate(flops=10**7, bytes_accessed=5 * 10**6, transcendentals=10**6),
    )(
        layer_pressure_depth,
        layer_thickness_fraction[None],
        cell_kelvin_field,
        daytime_indicator,
        kinetic_factor_times_step[None],
        arrhenius_barrier[None],
        species_yield_matrix,
        reagent_pairs,
    )
    reacted = kernel_call(
        functools.partial(column_kernel, (blocks, levels, species, pairs // 2)),
        "columns",
        arrays(packed.shape)[0],
        [(blocks // 2, mixed, LANES)] * 2,
    )(moved, *prepared)
    returned = lax.all_to_all(reacted, "lev", split_axis=0, concat_axis=0, tiled=True)
    out = kernel_call(
        functools.partial(spread_kernel, sizes),
        "spread",
        arrays((mixed * rows * parts, LANES))[0],
        [],
    )(returned)
    return out.reshape(species_fractions.shape)


def solution(mesh):
    placed = (
        P(None, "lev", "lat", None),
        P(None, "lev", "lat", None),
        P(None, "lat", "lev"),
        P(),
        P(None, "lat", "lev"),
        P(None, "lat", "lev"),
        P(),
        P(),
        P(),
        P(),
    )
    return jax.shard_map(
        body, mesh=mesh, in_specs=placed, out_specs=P(None, "lev", "lat", None), check_vma=False
    )
```

```python
import functools

import jax
import jax.numpy as jnp
from jax import lax
from jax.experimental import pallas as pl
from jax.experimental.pallas import tpu as pltpu
from jax.sharding import PartitionSpec as P

LANES = 128
PAD = 8
SWEEPS = 2
PARAMS = pltpu.CompilerParams(vmem_limit_bytes=16 * 2**20)
F32 = jnp.float32


def limited_slope(left, right):
    return jnp.maximum(jnp.minimum(left, right), 0.0) + jnp.minimum(jnp.maximum(left, right), 0.0)


def slope_weight(courant):
    return courant * (0.5 * (jnp.where(courant > 0.0, 1.0, -1.0) - courant))


def face_flux(courant, weight, before, after, before_slope, after_slope):
    ahead = courant > 0.0
    return courant * jnp.where(ahead, before, after) + weight * jnp.where(
        ahead, before_slope, after_slope
    )


def put_cyclic(ref, row, value):
    size = value.shape[0]
    ref[row, PAD : PAD + size] = value
    ref[row, PAD - 1 : PAD] = value[size - 1 :]
    ref[row, PAD + size : PAD + size + 1] = value[:1]


def shifted(ref, row, size, by):
    return ref[row, PAD + by : PAD + by + size]


def lon_step(f_ref, slope_ref, flux_ref, row, courant, weight):
    size = courant.shape[0]
    f, left, right = (shifted(f_ref, row, size, by) for by in (0, -1, 1))
    slope = limited_slope(f - left, right - f)
    put_cyclic(slope_ref, row, slope)
    flux = face_flux(courant, weight, left, f, shifted(slope_ref, row, size, -1), slope)
    put_cyclic(flux_ref, row, flux)
    return f - (shifted(flux_ref, row, size, 1) - flux)


def lat_step(f, weights):
    jumps = [f[i + 1] - f[i] for i in range(len(f) - 1)]
    slopes = [None] + [limited_slope(jumps[i - 1], jumps[i]) for i in range(1, len(f) - 1)]
    fluxes = [
        face_flux(*weights[i - 2], f[i - 1], f[i], slopes[i - 1], slopes[i])
        for i in range(2, len(f) - 1)
    ]
    return [f[i] - (fluxes[i - 1] - fluxes[i - 2]) for i in range(2, len(f) - 2)]


def tracer_rows(sizes, ref, row):
    species, levels, rows, parts, _ = sizes
    return [
        ref[pl.ds(row * parts + k, species * levels, rows * parts), :] for k in range(parts)
    ]


def flow_rows(sizes, ref, which, row):
    species, levels, rows, parts, _ = sizes
    found = []
    for k in range(parts):
        start = (which * levels * rows + row) * parts + k
        level_rows = ref[pl.ds(start, levels, rows * parts), :]
        tile = jnp.concatenate([level_rows] * (8 // levels), axis=0)
        found.append(jnp.concatenate([tile] * (species * levels // 8), axis=0))
    return found


def turned(tiles):
    return jnp.concatenate([tile.T for tile in tiles], axis=0)


def zonal_weights(flow_ref, row, flow):
    put_cyclic(flow_ref, row, flow)
    courant = 0.5 * (shifted(flow_ref, row, flow.shape[0], -1) + flow)
    return courant, slope_weight(courant)


def own_rows(
    sizes, band_ref, wind_ref, f_out, zonal_out, merid_out, f_ref, slope_ref, flux_ref, flow_ref
):
    rows = sizes[2]
    for row in range(rows):
        courant, weight = zonal_weights(
            flow_ref, row, turned(flow_rows(sizes, wind_ref, 0, row))
        )
        zonal_out[row, 0], zonal_out[row, 1] = courant, weight
        merid_out[row] = turned(flow_rows(sizes, wind_ref, 1, row))
        put_cyclic(f_ref, row, turned(tracer_rows(sizes, band_ref, row)))
        f_out[row] = lon_step(f_ref, slope_ref, flux_ref, row, courant, weight)


def advect_kernel(
    sizes,
    own_ref,
    own_zonal,
    own_merid,
    core_ref,
    chip_ref,
    core_wind,
    chip_wind,
    out_ref,
    f_ref,
    slope_ref,
    flux_ref,
    flow_ref,
    halo_zonal,
    halo_merid,
    merid_ref,
    next_ref,
):
    species, levels, rows, parts, width = sizes
    band = lax.axis_index("lat")
    even = band % 2 == 0

    def both_sides(by_core, by_chip):
        pairs = list(zip(by_core, by_chip, strict=True))
        before = [jnp.where(even, chip, core) for core, chip in pairs]
        after = [jnp.where(even, core, chip) for core, chip in pairs]
        return before, after

    for row in range(rows):
        zonal = both_sides(
            flow_rows(sizes, core_wind, 0, row), flow_rows(sizes, chip_wind, 0, row)
        )
        merid = both_sides(
            flow_rows(sizes, core_wind, 1, row), flow_rows(sizes, chip_wind, 1, row)
        )
        tracer = both_sides(
            tracer_rows(sizes, core_ref, row), tracer_rows(sizes, chip_ref, row)
        )
        for side in range(2):
            at = side * rows + row
            courant, weight = zonal_weights(flow_ref, at, turned(zonal[side]))
            halo_zonal[at, 0], halo_zonal[at, 1] = courant, weight
            halo_merid[at] = turned(merid[side])
            put_cyclic(f_ref, at, turned(tracer[side]))
            f_ref[at, PAD : PAD + courant.shape[0]] = lon_step(
                f_ref, slope_ref, flux_ref, at, courant, weight
            )

    def row_of(halo, own, row):
        if 0 <= row < rows:
            return own, row
        return halo, (row + rows if row < 0 else row)

    total = rows * lax.axis_size("lat")
    size = own_ref.shape[1]
    first_face, last_face = 2 - 2 * SWEEPS, rows + 2 * SWEEPS - 2
    for chunk in range(size // width):
        there = slice(chunk * width, (chunk + 1) * width)
        inner = slice(PAD + chunk * width, PAD + (chunk + 1) * width)

        def merid_at(row):
            ref, at = row_of(halo_merid, own_merid, row)
            return ref[at, there]

        weights = []
        for face in range(first_face, last_face + 1):
            place = band * rows + face
            open_face = jnp.logical_and(place >= 1, place <= total - 1).astype(F32)
            courant = 0.5 * (merid_at(face - 1) + merid_at(face)) * open_face
            weights.append((courant, slope_weight(courant)))
            if 0 <= face <= rows:
                merid_ref[face, 0, there], merid_ref[face, 1, there] = weights[-1]
        f = []
        for row in range(-rows, 2 * rows):
            ref, at = row_of(f_ref, own_ref, row)
            f.append(ref[at, there if ref is own_ref else inner])
        for at, value in enumerate(lat_step(f, weights)):
            next_ref[at, inner] = value

    swept = rows + 2 * SWEEPS
    for at in range(swept):
        next_ref[at, PAD - 1 : PAD] = next_ref[at, PAD + size - 1 : PAD + size]
        next_ref[at, PAD + size : PAD + size + 1] = next_ref[at, PAD : PAD + 1]
        ref, there = row_of(halo_zonal, own_zonal, at - 2)
        f_ref[at, PAD : PAD + size] = lon_step(
            next_ref, slope_ref, flux_ref, at, ref[there, 0], ref[there, 1]
        )
    for chunk in range(size // width):
        there = slice(chunk * width, (chunk + 1) * width)
        inner = slice(PAD + chunk * width, PAD + (chunk + 1) * width)
        f = [f_ref[at, inner] for at in range(swept)]
        weights = [
            (merid_ref[face, 0, there], merid_ref[face, 1, there]) for face in range(rows + 1)
        ]
        for row, value in enumerate(lat_step(f, weights)):
            out_ref[chunk, row * width : (row + 1) * width] = value


def spread_kernel(sizes, in_ref, out_ref):
    species, levels, rows, parts, width = sizes
    per_part = LANES // width
    for row in range(rows):
        for k in range(parts):
            found = [
                in_ref[k * per_part + j, row * width : (row + 1) * width] for j in range(per_part)
            ]
            out_ref[pl.ds(row * parts + k, species * levels, rows * parts), :] = jnp.concatenate(
                found, axis=0
            ).T


def paired(groups, ref, place):
    rows, width, all_levels = ref.shape
    by_level = ref[...].reshape(rows * width, all_levels).T
    levels = all_levels // groups
    for pair in range(groups // 2):
        for parity in range(2):
            start = (2 * pair + parity) * levels
            lane = parity * rows * width
            place[pair * levels : (pair + 1) * levels, lane : lane + rows * width] = by_level[
                start : start + levels
            ]


def early_kernel(sizes, groups, *refs):
    inputs, refs = refs[:10], refs[10:]
    outputs, refs = refs[:8], refs[8:]
    places, sems = refs[:10], refs[10]
    own_scratch, prepare_scratch = refs[11:15], refs[15:]
    copies = [
        pltpu.make_async_copy(source, place, sems.at[i])
        for i, (source, place) in enumerate(zip(inputs, places, strict=True))
    ]
    for copy in copies:
        copy.start()
    for copy in copies:
        copy.wait()
    own_rows(sizes, *places[:2], *outputs[:3], *own_scratch)
    prepare(groups, *places[2:], *outputs[3:], *prepare_scratch)


def prepare(
    groups,
    depth_ref,
    share_ref,
    kelvin_ref,
    active_ref,
    factor_ref,
    barrier_ref,
    yield_ref,
    pair_ref,
    overlap_out,
    rate_out,
    active_out,
    pick_out,
    yield_out,
    depth_at,
    kelvin_at,
    lower_at,
):
    rows, width, all_levels = depth_ref.shape
    levels = all_levels // groups
    half = LANES // 2
    odd = lax.broadcasted_iota(jnp.int32, (1, LANES), 1) >= half
    species, reactions = yield_ref.shape

    paired(groups, kelvin_ref, kelvin_at)
    paired(groups, depth_ref, depth_at)
    for parity in range(2):
        for row in range(rows):
            lane = (parity * rows + row) * width
            active_out[:, lane : lane + width] = active_ref[:, row, :]

    def column(ref):
        return jnp.broadcast_to(ref[...], (LANES, ref.shape[1])).T

    base = jnp.zeros((1, LANES), F32)
    for pair in range(groups // 2):
        inside = jnp.zeros((1, LANES), F32)
        for level in range(levels):
            at = pair * levels + level
            lower_at[at : at + 1] = inside
            inside = inside + depth_at[at : at + 1]
        other = pltpu.roll(inside, half, 1)
        start = base + jnp.where(odd, other, 0.0)
        here = slice(pair * levels, (pair + 1) * levels)
        lower_at[here] = lower_at[here] + start
        base = base + (inside + other)
    total = base
    lower = lower_at[...]
    upper = lower + depth_at[...]

    share = column(share_ref)
    share_sum = share[0:1]
    for t in range(1, all_levels):
        share_sum = share_sum + share[t : t + 1]
    below = jnp.zeros((1, LANES), F32)
    target_low = below
    for t in range(all_levels):
        below = below + share[t : t + 1]
        target_top = below / share_sum * total
        shared = jnp.maximum(
            jnp.minimum(upper, target_top) - jnp.maximum(lower, target_low), 0.0
        )
        overlap_out[t] = shared / (share[t : t + 1] / share_sum * total)
        target_low = target_top

    factor, barrier = column(factor_ref), column(barrier_ref)
    for at in range(kelvin_at.shape[0]):
        warmth = 300.0 / kelvin_at[at : at + 1] - 1.0
        rate_out[:, at * LANES : (at + 1) * LANES] = factor * jnp.exp(-barrier * warmth)

    one_species = lax.broadcasted_iota(jnp.int32, (2 * species, reactions), 0) % species
    for which in range(2):
        hit = (one_species == pair_ref[which : which + 1, :]).astype(F32)
        pick_out[which * reactions : (which + 1) * reactions] = hit.T.astype(jnp.bfloat16)
    yields = yield_ref[...].astype(F32).astype(jnp.bfloat16)
    yield_out[:, :reactions] = yields
    yield_out[:, reactions:] = yields


def in_two_parts(value):
    high = value.astype(jnp.bfloat16)
    low = (value - high.astype(F32)).astype(jnp.bfloat16)
    return jnp.concatenate([high, low], axis=0)


def column_kernel(
    sizes,
    moved_ref,
    overlap_ref,
    rate_ref,
    active_ref,
    pick_ref,
    yield_ref,
    out_ref,
    source_ref,
    target_ref,
):
    groups, levels, species, tile_pairs = sizes
    half = LANES // 2
    pairs = groups // 2 * levels
    reactions = yield_ref.shape[1] // 2
    odd = lax.broadcasted_iota(jnp.int32, (1, LANES), 1) >= half

    for pair in range(groups // 2):
        both = jnp.concatenate([moved_ref[2 * pair], moved_ref[2 * pair + 1]], axis=0)
        source_ref[pair] = both.T

    def remapped(at):
        pair, level = divmod(at, levels)
        sums = []
        for parity in range(2):
            t = (2 * pair + parity) * levels + level
            acc = None
            for s in range(pairs):
                source = source_ref[s // levels, pl.ds(s % levels, species, levels), :]
                term = overlap_ref[t, s : s + 1, :] * source
                acc = term if acc is None else acc + term
            sums.append(acc)
        kept = jnp.where(odd, sums[1], sums[0])
        crossed = jnp.where(odd, sums[0], sums[1])
        return kept + pltpu.roll(crossed, half, 1)

    tiles = [range(first, first + tile_pairs) for first in range(0, pairs, tile_pairs)]
    q = [jnp.concatenate([remapped(at) for at in tile], axis=1) for tile in tiles]
    for substep in range(active_ref.shape[0]):
        on = jnp.concatenate([active_ref[substep : substep + 1, :]] * tile_pairs, axis=1) > 0
        picked = [
            jnp.dot(pick_ref[...], in_two_parts(value), preferred_element_type=F32) for value in q
        ]
        rates = [
            rate_ref[:, tile[0] * LANES : (tile[-1] + 1) * LANES]
            * found[:reactions]
            * found[reactions:]
            for tile, found in zip(tiles, picked, strict=True)
        ]
        rates = [in_two_parts(value) for value in rates]
        changes = [
            jnp.dot(yield_ref[...], value, preferred_element_type=F32) for value in rates
        ]
        q = [
            jnp.where(on, value + change, value) for value, change in zip(q, changes, strict=True)
        ]
    for tile, value in zip(tiles, q, strict=True):
        for inside, at in enumerate(tile):
            pair, level = divmod(at, levels)
            lane = inside * LANES
            target_ref[pair, pl.ds(level, species, levels), :] = value[:, lane : lane + LANES]

    for pair in range(groups // 2):
        both = target_ref[pair].T
        out_ref[2 * pair], out_ref[2 * pair + 1] = both[:half], both[half:]


def swap_pairs(count, first):
    route = []
    for low in range(first, count - 1, 2):
        route += [(low, low + 1), (low + 1, low)]
    return route


def kernel_call(kernel, name, outs, scratch, cost=None):
    return pl.pallas_call(
        kernel,
        out_shape=outs,
        scratch_shapes=[pltpu.VMEM(shape, F32) for shape in scratch],
        compiler_params=PARAMS,
        cost_estimate=cost,
        name=name,
    )


def body(
    species_fractions,
    cell_flow_ratios,
    layer_pressure_depth,
    layer_thickness_fraction,
    cell_kelvin_field,
    daytime_indicator,
    kinetic_factor_times_step,
    arrhenius_barrier,
    species_yield_matrix,
    reagent_pairs,
):
    species, levels, rows, lons = species_fractions.shape
    all_levels = layer_pressure_depth.shape[0]
    width = layer_pressure_depth.shape[2]
    blocks = lax.axis_size("lev")
    bands = lax.axis_size("lat")
    parts = lons // LANES
    substeps = daytime_indicator.shape[0]
    reactions = kinetic_factor_times_step.shape[0]
    assert 2 * rows * width == LANES and rows == 2 * SWEEPS and blocks % 2 == 0
    sizes = (species, levels, rows, parts, width)
    mixed = species * levels

    by_core, by_chip = swap_pairs(bands, 0), swap_pairs(bands, 1)
    core_band = lax.ppermute(species_fractions, "lat", by_core)
    chip_band = lax.ppermute(species_fractions, "lat", by_chip)
    core_wind = lax.ppermute(cell_flow_ratios, "lat", by_core)
    chip_wind = lax.ppermute(cell_flow_ratios, "lat", by_chip)

    def flat(value):
        return value.reshape(-1, LANES)

    def arrays(*shapes):
        return [jax.ShapeDtypeStruct(shape, F32) for shape in shapes]

    padded = lons + 2 * PAD
    pairs = all_levels // 2
    operands = (
        flat(species_fractions),
        flat(cell_flow_ratios),
        layer_pressure_depth.transpose(1, 2, 0),
        layer_thickness_fraction[None],
        cell_kelvin_field.transpose(1, 2, 0),
        daytime_indicator,
        kinetic_factor_times_step[None],
        arrhenius_barrier[None],
        species_yield_matrix.T,
        reagent_pairs,
    )
    early = pl.pallas_call(
        functools.partial(early_kernel, sizes, blocks),
        out_shape=[
            *arrays((rows, lons, mixed), (rows, 2, lons, mixed), (rows, lons, mixed)),
            *arrays((all_levels, pairs, LANES), (reactions, pairs * LANES)),
            jax.ShapeDtypeStruct((substeps, LANES), jnp.int32),
            jax.ShapeDtypeStruct((2 * reactions, 2 * species), jnp.bfloat16),
            jax.ShapeDtypeStruct((species, 2 * reactions), jnp.bfloat16),
        ],
        in_specs=[pl.BlockSpec(memory_space=pltpu.HBM)] * len(operands),
        scratch_shapes=[
            *[pltpu.VMEM(item.shape, item.dtype) for item in operands],
            pltpu.SemaphoreType.DMA((len(operands),)),
            *[pltpu.VMEM((rows, padded, mixed), F32)] * 4,
            *[pltpu.VMEM((pairs, LANES), F32)] * 3,
        ],
        compiler_params=PARAMS,
        cost_estimate=pl.CostEstimate(
            flops=10**7, bytes_accessed=7 * 10**6, transcendentals=10**6
        ),
        name="early",
    )(*[pltpu.with_memory_space_constraint(item, pltpu.HBM) for item in operands])
    own, prepared = early[:3], early[3:]

    packed = kernel_call(
        functools.partial(advect_kernel, sizes),
        "advect",
        arrays((blocks, rows * width, mixed))[0],
        [(2 * rows, padded, mixed)] * 4
        + [
            (2 * rows, 2, lons, mixed),
            (2 * rows, lons, mixed),
            (rows + 1, 2, lons, mixed),
            (2 * rows, padded, mixed),
        ],
    )(*own, flat(core_band), flat(chip_band), flat(core_wind), flat(chip_wind))
    moved = lax.all_to_all(packed, "lev", split_axis=0, concat_axis=0, tiled=True)

    reacted = kernel_call(
        functools.partial(column_kernel, (blocks, levels, species, pairs // 4)),
        "columns",
        arrays(packed.shape)[0],
        [(blocks // 2, mixed, LANES)] * 2,
    )(moved, *prepared)
    returned = lax.all_to_all(reacted, "lev", split_axis=0, concat_axis=0, tiled=True)
    out = kernel_call(
        functools.partial(spread_kernel, sizes),
        "spread",
        arrays((mixed * rows * parts, LANES))[0],
        [],
    )(returned)
    return out.reshape(species_fractions.shape)


def solution(mesh):
    placed = (
        P(None, "lev", "lat", None),
        P(None, "lev", "lat", None),
        P(None, "lat", "lev"),
        P(),
        P(None, "lat", "lev"),
        P(None, "lat", "lev"),
        P(),
        P(),
        P(),
        P(),
    )
    return jax.shard_map(
        body, mesh=mesh, in_specs=placed, out_specs=P(None, "lev", "lat", None), check_vma=False
    )
```

```python
import functools

import jax
import jax.numpy as jnp
from jax import lax
from jax.experimental import pallas as pl
from jax.experimental.pallas import tpu as pltpu
from jax.sharding import PartitionSpec as P

LANES = 128
PAD = 8
SWEEPS = 2
PARAMS = pltpu.CompilerParams(vmem_limit_bytes=16 * 2**20)
F32 = jnp.float32


def limited_slope(left, right):
    return jnp.maximum(jnp.minimum(left, right), 0.0) + jnp.minimum(jnp.maximum(left, right), 0.0)


def slope_weight(courant):
    return courant * (0.5 * (jnp.where(courant > 0.0, 1.0, -1.0) - courant))


def face_flux(courant, weight, before, after, before_slope, after_slope):
    ahead = courant > 0.0
    return courant * jnp.where(ahead, before, after) + weight * jnp.where(
        ahead, before_slope, after_slope
    )


def put_cyclic(ref, row, value):
    size = value.shape[0]
    ref[row, PAD : PAD + size] = value
    ref[row, PAD - 1 : PAD] = value[size - 1 :]
    ref[row, PAD + size : PAD + size + 1] = value[:1]


def shifted(ref, row, size, by):
    return ref[row, PAD + by : PAD + by + size]


def lon_step(f_ref, slope_ref, flux_ref, row, courant, weight):
    size = courant.shape[0]
    f, left, right = (shifted(f_ref, row, size, by) for by in (0, -1, 1))
    slope = limited_slope(f - left, right - f)
    put_cyclic(slope_ref, row, slope)
    flux = face_flux(courant, weight, left, f, shifted(slope_ref, row, size, -1), slope)
    put_cyclic(flux_ref, row, flux)
    return f - (shifted(flux_ref, row, size, 1) - flux)


def lat_step(f, weights):
    jumps = [f[i + 1] - f[i] for i in range(len(f) - 1)]
    slopes = [None] + [limited_slope(jumps[i - 1], jumps[i]) for i in range(1, len(f) - 1)]
    fluxes = [
        face_flux(*weights[i - 2], f[i - 1], f[i], slopes[i - 1], slopes[i])
        for i in range(2, len(f) - 1)
    ]
    return [f[i] - (fluxes[i - 1] - fluxes[i - 2]) for i in range(2, len(f) - 2)]


def tracer_rows(sizes, ref, row):
    species, levels, rows, parts, _ = sizes
    return [
        ref[pl.ds(row * parts + k, species * levels, rows * parts), :] for k in range(parts)
    ]


def flow_rows(sizes, ref, which, row, skip=0):
    species, levels, rows, parts, _ = sizes
    found = []
    for k in range(parts):
        start = ((skip + which) * levels * rows + row) * parts + k
        level_rows = ref[pl.ds(start, levels, rows * parts), :]
        tile = jnp.concatenate([level_rows] * (8 // levels), axis=0)
        found.append(jnp.concatenate([tile] * (species * levels // 8), axis=0))
    return found


def turned(tiles):
    return jnp.concatenate([tile.T for tile in tiles], axis=0)


def zonal_weights(flow_ref, row, flow):
    put_cyclic(flow_ref, row, flow)
    courant = 0.5 * (shifted(flow_ref, row, flow.shape[0], -1) + flow)
    return courant, slope_weight(courant)


def own_rows(
    sizes, sent_ref, f_out, zonal_out, merid_out, f_ref, slope_ref, flux_ref, flow_ref
):
    species, rows = sizes[0], sizes[2]
    for row in range(rows):
        courant, weight = zonal_weights(
            flow_ref, row, turned(flow_rows(sizes, sent_ref, 0, row, species))
        )
        zonal_out[row, 0], zonal_out[row, 1] = courant, weight
        merid_out[row] = turned(flow_rows(sizes, sent_ref, 1, row, species))
        put_cyclic(f_ref, row, turned(tracer_rows(sizes, sent_ref, row)))
        f_out[row] = lon_step(f_ref, slope_ref, flux_ref, row, courant, weight)


def advect_kernel(
    sizes,
    own_ref,
    own_zonal,
    own_merid,
    core_ref,
    chip_ref,
    out_ref,
    f_ref,
    slope_ref,
    flux_ref,
    flow_ref,
    halo_zonal,
    halo_merid,
    merid_ref,
    next_ref,
):
    species, levels, rows, parts, width = sizes
    band = lax.axis_index("lat")
    even = band % 2 == 0

    def both_sides(by_core, by_chip):
        pairs = list(zip(by_core, by_chip, strict=True))
        before = [jnp.where(even, chip, core) for core, chip in pairs]
        after = [jnp.where(even, core, chip) for core, chip in pairs]
        return before, after

    for row in range(rows):
        zonal = both_sides(
            flow_rows(sizes, core_ref, 0, row, species), flow_rows(sizes, chip_ref, 0, row, species)
        )
        merid = both_sides(
            flow_rows(sizes, core_ref, 1, row, species), flow_rows(sizes, chip_ref, 1, row, species)
        )
        tracer = both_sides(
            tracer_rows(sizes, core_ref, row), tracer_rows(sizes, chip_ref, row)
        )
        for side in range(2):
            at = side * rows + row
            courant, weight = zonal_weights(flow_ref, at, turned(zonal[side]))
            halo_zonal[at, 0], halo_zonal[at, 1] = courant, weight
            halo_merid[at] = turned(merid[side])
            put_cyclic(f_ref, at, turned(tracer[side]))
            f_ref[at, PAD : PAD + courant.shape[0]] = lon_step(
                f_ref, slope_ref, flux_ref, at, courant, weight
            )

    def row_of(halo, own, row):
        if 0 <= row < rows:
            return own, row
        return halo, (row + rows if row < 0 else row)

    total = rows * lax.axis_size("lat")
    size = own_ref.shape[1]
    first_face, last_face = 2 - 2 * SWEEPS, rows + 2 * SWEEPS - 2
    for chunk in range(size // width):
        there = slice(chunk * width, (chunk + 1) * width)
        inner = slice(PAD + chunk * width, PAD + (chunk + 1) * width)

        def merid_at(row):
            ref, at = row_of(halo_merid, own_merid, row)
            return ref[at, there]

        weights = []
        for face in range(first_face, last_face + 1):
            place = band * rows + face
            open_face = jnp.logical_and(place >= 1, place <= total - 1).astype(F32)
            courant = 0.5 * (merid_at(face - 1) + merid_at(face)) * open_face
            weights.append((courant, slope_weight(courant)))
            if 0 <= face <= rows:
                merid_ref[face, 0, there], merid_ref[face, 1, there] = weights[-1]
        f = []
        for row in range(-rows, 2 * rows):
            ref, at = row_of(f_ref, own_ref, row)
            f.append(ref[at, there if ref is own_ref else inner])
        for at, value in enumerate(lat_step(f, weights)):
            next_ref[at, inner] = value

    swept = rows + 2 * SWEEPS
    for at in range(swept):
        next_ref[at, PAD - 1 : PAD] = next_ref[at, PAD + size - 1 : PAD + size]
        next_ref[at, PAD + size : PAD + size + 1] = next_ref[at, PAD : PAD + 1]
        ref, there = row_of(halo_zonal, own_zonal, at - 2)
        f_ref[at, PAD : PAD + size] = lon_step(
            next_ref, slope_ref, flux_ref, at, ref[there, 0], ref[there, 1]
        )
    for chunk in range(size // width):
        there = slice(chunk * width, (chunk + 1) * width)
        inner = slice(PAD + chunk * width, PAD + (chunk + 1) * width)
        f = [f_ref[at, inner] for at in range(swept)]
        weights = [
            (merid_ref[face, 0, there], merid_ref[face, 1, there]) for face in range(rows + 1)
        ]
        for row, value in enumerate(lat_step(f, weights)):
            out_ref[chunk, row * width : (row + 1) * width] = value


def spread_kernel(sizes, in_ref, out_ref):
    species, levels, rows, parts, width = sizes
    per_part = LANES // width
    for row in range(rows):
        for k in range(parts):
            found = [
                in_ref[k * per_part + j, row * width : (row + 1) * width] for j in range(per_part)
            ]
            out_ref[pl.ds(row * parts + k, species * levels, rows * parts), :] = jnp.concatenate(
                found, axis=0
            ).T


def paired(groups, ref, place):
    rows, width, all_levels = ref.shape
    by_level = ref[...].reshape(rows * width, all_levels).T
    levels = all_levels // groups
    for pair in range(groups // 2):
        for parity in range(2):
            start = (2 * pair + parity) * levels
            lane = parity * rows * width
            place[pair * levels : (pair + 1) * levels, lane : lane + rows * width] = by_level[
                start : start + levels
            ]


def pack_kernel(tracer_ref, wind_ref, out_ref, sems):
    size = tracer_ref.shape[0]
    copies = [
        pltpu.make_async_copy(tracer_ref, out_ref.at[:size], sems.at[0]),
        pltpu.make_async_copy(wind_ref, out_ref.at[size:], sems.at[1]),
    ]
    for copy in copies:
        copy.start()
    for copy in copies:
        copy.wait()


def early_kernel(sizes, groups, *refs):
    sent_ref, inputs, refs = refs[0], refs[1:9], refs[9:]
    outputs, refs = refs[:8], refs[8:]
    places, sems = refs[:8], refs[8]
    own_scratch, prepare_scratch = refs[9:13], refs[13:]
    copies = [
        pltpu.make_async_copy(source, place, sems.at[i])
        for i, (source, place) in enumerate(zip(inputs, places, strict=True))
    ]
    for copy in copies:
        copy.start()
    own_rows(sizes, sent_ref, *outputs[:3], *own_scratch)
    for copy in copies:
        copy.wait()
    prepare(groups, *places, *outputs[3:], *prepare_scratch)


def prepare(
    groups,
    depth_ref,
    share_ref,
    kelvin_ref,
    active_ref,
    factor_ref,
    barrier_ref,
    yield_ref,
    pair_ref,
    overlap_out,
    rate_out,
    active_out,
    pick_out,
    yield_out,
    depth_at,
    kelvin_at,
    lower_at,
):
    rows, width, all_levels = depth_ref.shape
    levels = all_levels // groups
    half = LANES // 2
    odd = lax.broadcasted_iota(jnp.int32, (1, LANES), 1) >= half
    species, reactions = yield_ref.shape

    paired(groups, kelvin_ref, kelvin_at)
    paired(groups, depth_ref, depth_at)
    for parity in range(2):
        for row in range(rows):
            lane = (parity * rows + row) * width
            active_out[:, lane : lane + width] = active_ref[:, row, :]

    def column(ref):
        return jnp.broadcast_to(ref[...], (LANES, ref.shape[1])).T

    base = jnp.zeros((1, LANES), F32)
    for pair in range(groups // 2):
        inside = jnp.zeros((1, LANES), F32)
        for level in range(levels):
            at = pair * levels + level
            lower_at[at : at + 1] = inside
            inside = inside + depth_at[at : at + 1]
        other = pltpu.roll(inside, half, 1)
        start = base + jnp.where(odd, other, 0.0)
        here = slice(pair * levels, (pair + 1) * levels)
        lower_at[here] = lower_at[here] + start
        base = base + (inside + other)
    total = base
    lower = lower_at[...]
    upper = lower + depth_at[...]

    share = column(share_ref)
    share_sum = share[0:1]
    for t in range(1, all_levels):
        share_sum = share_sum + share[t : t + 1]
    below = jnp.zeros((1, LANES), F32)
    target_low = below
    for t in range(all_levels):
        below = below + share[t : t + 1]
        target_top = below / share_sum * total
        shared = jnp.maximum(
            jnp.minimum(upper, target_top) - jnp.maximum(lower, target_low), 0.0
        )
        overlap_out[t] = shared / (share[t : t + 1] / share_sum * total)
        target_low = target_top

    factor, barrier = column(factor_ref), column(barrier_ref)
    for at in range(kelvin_at.shape[0]):
        warmth = 300.0 / kelvin_at[at : at + 1] - 1.0
        rate_out[:, at * LANES : (at + 1) * LANES] = factor * jnp.exp(-barrier * warmth)

    one_species = lax.broadcasted_iota(jnp.int32, (2 * species, reactions), 0) % species
    for which in range(2):
        hit = (one_species == pair_ref[which : which + 1, :]).astype(F32)
        pick_out[which * reactions : (which + 1) * reactions] = hit.T.astype(jnp.bfloat16)
    yields = yield_ref[...].astype(F32).astype(jnp.bfloat16)
    yield_out[:, :reactions] = yields
    yield_out[:, reactions:] = yields


def in_two_parts(value):
    high = value.astype(jnp.bfloat16)
    low = (value - high.astype(F32)).astype(jnp.bfloat16)
    return jnp.concatenate([high, low], axis=0)


def column_kernel(
    sizes,
    moved_ref,
    overlap_ref,
    rate_ref,
    active_ref,
    pick_ref,
    yield_ref,
    out_ref,
    source_ref,
    target_ref,
):
    groups, levels, species, tile_pairs = sizes
    half = LANES // 2
    pairs = groups // 2 * levels
    reactions = yield_ref.shape[1] // 2
    odd = lax.broadcasted_iota(jnp.int32, (1, LANES), 1) >= half

    for pair in range(groups // 2):
        both = jnp.concatenate([moved_ref[2 * pair], moved_ref[2 * pair + 1]], axis=0)
        source_ref[pair] = both.T

    def remapped(at):
        pair, level = divmod(at, levels)
        sums = []
        for parity in range(2):
            t = (2 * pair + parity) * levels + level
            acc = None
            for s in range(pairs):
                source = source_ref[s // levels, pl.ds(s % levels, species, levels), :]
                term = overlap_ref[t, s : s + 1, :] * source
                acc = term if acc is None else acc + term
            sums.append(acc)
        kept = jnp.where(odd, sums[1], sums[0])
        crossed = jnp.where(odd, sums[0], sums[1])
        return kept + pltpu.roll(crossed, half, 1)

    tiles = [range(first, first + tile_pairs) for first in range(0, pairs, tile_pairs)]
    q = [jnp.concatenate([remapped(at) for at in tile], axis=1) for tile in tiles]
    for substep in range(active_ref.shape[0]):
        on = jnp.concatenate([active_ref[substep : substep + 1, :]] * tile_pairs, axis=1) > 0
        picked = [
            jnp.dot(pick_ref[...], in_two_parts(value), preferred_element_type=F32) for value in q
        ]
        rates = [
            rate_ref[:, tile[0] * LANES : (tile[-1] + 1) * LANES]
            * found[:reactions]
            * found[reactions:]
            for tile, found in zip(tiles, picked, strict=True)
        ]
        rates = [in_two_parts(value) for value in rates]
        changes = [
            jnp.dot(yield_ref[...], value, preferred_element_type=F32) for value in rates
        ]
        q = [
            jnp.where(on, value + change, value) for value, change in zip(q, changes, strict=True)
        ]
    for tile, value in zip(tiles, q, strict=True):
        for inside, at in enumerate(tile):
            pair, level = divmod(at, levels)
            lane = inside * LANES
            target_ref[pair, pl.ds(level, species, levels), :] = value[:, lane : lane + LANES]

    for pair in range(groups // 2):
        both = target_ref[pair].T
        out_ref[2 * pair], out_ref[2 * pair + 1] = both[:half], both[half:]


def swap_pairs(count, first):
    route = []
    for low in range(first, count - 1, 2):
        route += [(low, low + 1), (low + 1, low)]
    return route


def kernel_call(kernel, name, outs, scratch, cost=None):
    return pl.pallas_call(
        kernel,
        out_shape=outs,
        scratch_shapes=[pltpu.VMEM(shape, F32) for shape in scratch],
        compiler_params=PARAMS,
        cost_estimate=cost,
        name=name,
    )


def body(
    species_fractions,
    cell_flow_ratios,
    layer_pressure_depth,
    layer_thickness_fraction,
    cell_kelvin_field,
    daytime_indicator,
    kinetic_factor_times_step,
    arrhenius_barrier,
    species_yield_matrix,
    reagent_pairs,
):
    species, levels, rows, lons = species_fractions.shape
    all_levels = layer_pressure_depth.shape[0]
    width = layer_pressure_depth.shape[2]
    blocks = lax.axis_size("lev")
    bands = lax.axis_size("lat")
    parts = lons // LANES
    substeps = daytime_indicator.shape[0]
    reactions = kinetic_factor_times_step.shape[0]
    assert 2 * rows * width == LANES and rows == 2 * SWEEPS and blocks % 2 == 0
    sizes = (species, levels, rows, parts, width)
    mixed = species * levels

    by_core, by_chip = swap_pairs(bands, 0), swap_pairs(bands, 1)
    def flat(value):
        return value.reshape(-1, LANES)

    def in_hbm(*values):
        return [pltpu.with_memory_space_constraint(item, pltpu.HBM) for item in values]

    tracers, winds = flat(species_fractions), flat(cell_flow_ratios)
    sent = pl.pallas_call(
        pack_kernel,
        out_shape=jax.ShapeDtypeStruct((len(tracers) + len(winds), LANES), F32),
        in_specs=[pl.BlockSpec(memory_space=pltpu.HBM)] * 2,
        scratch_shapes=[pltpu.SemaphoreType.DMA((2,))],
        compiler_params=PARAMS,
        name="pack",
    )(*in_hbm(tracers, winds))
    core_band = lax.ppermute(sent, "lat", by_core)
    chip_band = lax.ppermute(sent, "lat", by_chip)

    def arrays(*shapes):
        return [jax.ShapeDtypeStruct(shape, F32) for shape in shapes]

    padded = lons + 2 * PAD
    pairs = all_levels // 2
    operands = (
        layer_pressure_depth.transpose(1, 2, 0),
        layer_thickness_fraction[None],
        cell_kelvin_field.transpose(1, 2, 0),
        daytime_indicator,
        kinetic_factor_times_step[None],
        arrhenius_barrier[None],
        species_yield_matrix.T,
        reagent_pairs,
    )
    early = pl.pallas_call(
        functools.partial(early_kernel, sizes, blocks),
        out_shape=[
            *arrays((rows, lons, mixed), (rows, 2, lons, mixed), (rows, lons, mixed)),
            *arrays((all_levels, pairs, LANES), (reactions, pairs * LANES)),
            jax.ShapeDtypeStruct((substeps, LANES), jnp.int32),
            jax.ShapeDtypeStruct((2 * reactions, 2 * species), jnp.bfloat16),
            jax.ShapeDtypeStruct((species, 2 * reactions), jnp.bfloat16),
        ],
        in_specs=[pl.BlockSpec(memory_space=pltpu.VMEM)]
        + [pl.BlockSpec(memory_space=pltpu.HBM)] * len(operands),
        scratch_shapes=[
            *[pltpu.VMEM(item.shape, item.dtype) for item in operands],
            pltpu.SemaphoreType.DMA((len(operands),)),
            *[pltpu.VMEM((rows, padded, mixed), F32)] * 4,
            *[pltpu.VMEM((pairs, LANES), F32)] * 3,
        ],
        compiler_params=PARAMS,
        cost_estimate=pl.CostEstimate(
            flops=10**7, bytes_accessed=7 * 10**6, transcendentals=10**6
        ),
        name="early",
    )(sent, *in_hbm(*operands))
    own, prepared = early[:3], early[3:]

    packed = kernel_call(
        functools.partial(advect_kernel, sizes),
        "advect",
        arrays((blocks, rows * width, mixed))[0],
        [(2 * rows, padded, mixed)] * 4
        + [
            (2 * rows, 2, lons, mixed),
            (2 * rows, lons, mixed),
            (rows + 1, 2, lons, mixed),
            (2 * rows, padded, mixed),
        ],
    )(*own, core_band, chip_band)
    moved = lax.all_to_all(packed, "lev", split_axis=0, concat_axis=0, tiled=True)

    reacted = kernel_call(
        functools.partial(column_kernel, (blocks, levels, species, pairs // 4)),
        "columns",
        arrays(packed.shape)[0],
        [(blocks // 2, mixed, LANES)] * 2,
    )(moved, *prepared)
    returned = lax.all_to_all(reacted, "lev", split_axis=0, concat_axis=0, tiled=True)
    out = kernel_call(
        functools.partial(spread_kernel, sizes),
        "spread",
        arrays((mixed * rows * parts, LANES))[0],
        [],
    )(returned)
    return out.reshape(species_fractions.shape)


def solution(mesh):
    placed = (
        P(None, "lev", "lat", None),
        P(None, "lev", "lat", None),
        P(None, "lat", "lev"),
        P(),
        P(None, "lat", "lev"),
        P(None, "lat", "lev"),
        P(),
        P(),
        P(),
        P(),
    )
    return jax.shard_map(
        body, mesh=mesh, in_specs=placed, out_specs=P(None, "lev", "lat", None), check_vma=False
    )
```

```python
import functools

import jax
import jax.numpy as jnp
from jax import lax
from jax.experimental import pallas as pl
from jax.experimental.pallas import tpu as pltpu
from jax.sharding import PartitionSpec as P

LANES = 128
PAD = 8
SWEEPS = 2
PARAMS = pltpu.CompilerParams(vmem_limit_bytes=16 * 2**20)
F32 = jnp.float32


def limited_slope(left, right):
    return jnp.maximum(jnp.minimum(left, right), 0.0) + jnp.minimum(jnp.maximum(left, right), 0.0)


def slope_weight(courant):
    return courant * (0.5 * (jnp.where(courant > 0.0, 1.0, -1.0) - courant))


def face_flux(courant, weight, before, after, before_slope, after_slope):
    ahead = courant > 0.0
    return courant * jnp.where(ahead, before, after) + weight * jnp.where(
        ahead, before_slope, after_slope
    )


def put_cyclic(ref, row, value):
    size = value.shape[0]
    ref[row, PAD : PAD + size] = value
    ref[row, PAD - 1 : PAD] = value[size - 1 :]
    ref[row, PAD + size : PAD + size + 1] = value[:1]


def shifted(ref, row, size, by):
    return ref[row, PAD + by : PAD + by + size]


def lon_step(f_ref, slope_ref, flux_ref, row, courant, weight):
    size = courant.shape[0]
    f, left, right = (shifted(f_ref, row, size, by) for by in (0, -1, 1))
    slope = limited_slope(f - left, right - f)
    put_cyclic(slope_ref, row, slope)
    flux = face_flux(courant, weight, left, f, shifted(slope_ref, row, size, -1), slope)
    put_cyclic(flux_ref, row, flux)
    return f - (shifted(flux_ref, row, size, 1) - flux)


def lat_step(f, weights):
    jumps = [f[i + 1] - f[i] for i in range(len(f) - 1)]
    slopes = [None] + [limited_slope(jumps[i - 1], jumps[i]) for i in range(1, len(f) - 1)]
    fluxes = [
        face_flux(*weights[i - 2], f[i - 1], f[i], slopes[i - 1], slopes[i])
        for i in range(2, len(f) - 1)
    ]
    return [f[i] - (fluxes[i - 1] - fluxes[i - 2]) for i in range(2, len(f) - 2)]


def tracer_rows(sizes, ref, row):
    species, levels, rows, parts, _ = sizes
    return [
        ref[pl.ds(row * parts + k, species * levels, rows * parts), :] for k in range(parts)
    ]


def flow_rows(sizes, ref, which, row, skip=0):
    species, levels, rows, parts, _ = sizes
    found = []
    for k in range(parts):
        start = ((skip + which) * levels * rows + row) * parts + k
        level_rows = ref[pl.ds(start, levels, rows * parts), :]
        tile = jnp.concatenate([level_rows] * (8 // levels), axis=0)
        found.append(jnp.concatenate([tile] * (species * levels // 8), axis=0))
    return found


def turned(tiles):
    return jnp.concatenate([tile.T for tile in tiles], axis=0)


def zonal_weights(flow_ref, row, flow):
    put_cyclic(flow_ref, row, flow)
    courant = 0.5 * (shifted(flow_ref, row, flow.shape[0], -1) + flow)
    return courant, slope_weight(courant)


def own_rows(
    sizes, sent_ref, f_out, zonal_out, merid_out, f_ref, slope_ref, flux_ref, flow_ref
):
    species, rows = sizes[0], sizes[2]
    for row in range(rows):
        courant, weight = zonal_weights(
            flow_ref, row, turned(flow_rows(sizes, sent_ref, 0, row, species))
        )
        zonal_out[row, 0], zonal_out[row, 1] = courant, weight
        merid_out[row] = turned(flow_rows(sizes, sent_ref, 1, row, species))
        put_cyclic(f_ref, row, turned(tracer_rows(sizes, sent_ref, row)))
        f_out[row] = lon_step(f_ref, slope_ref, flux_ref, row, courant, weight)


def advect_kernel(
    sizes,
    own_ref,
    own_zonal,
    own_merid,
    chip_ref,
    core_ref,
    out_ref,
    f_ref,
    slope_ref,
    flux_ref,
    flow_ref,
    halo_zonal,
    halo_merid,
    merid_ref,
    next_ref,
):
    species, levels, rows, parts, width = sizes
    band = lax.axis_index("lat")
    even = band % 2 == 0

    def both_sides(by_core, by_chip):
        pairs = list(zip(by_core, by_chip, strict=True))
        before = [jnp.where(even, chip, core) for core, chip in pairs]
        after = [jnp.where(even, core, chip) for core, chip in pairs]
        return before, after

    for row in range(rows):
        zonal = both_sides(
            flow_rows(sizes, core_ref, 0, row, species), flow_rows(sizes, chip_ref, 0, row, species)
        )
        merid = both_sides(
            flow_rows(sizes, core_ref, 1, row, species), flow_rows(sizes, chip_ref, 1, row, species)
        )
        tracer = both_sides(
            tracer_rows(sizes, core_ref, row), tracer_rows(sizes, chip_ref, row)
        )
        for side in range(2):
            at = side * rows + row
            courant, weight = zonal_weights(flow_ref, at, turned(zonal[side]))
            halo_zonal[at, 0], halo_zonal[at, 1] = courant, weight
            halo_merid[at] = turned(merid[side])
            put_cyclic(f_ref, at, turned(tracer[side]))
            f_ref[at, PAD : PAD + courant.shape[0]] = lon_step(
                f_ref, slope_ref, flux_ref, at, courant, weight
            )

    def row_of(halo, own, row):
        if 0 <= row < rows:
            return own, row
        return halo, (row + rows if row < 0 else row)

    total = rows * lax.axis_size("lat")
    size = own_ref.shape[1]
    first_face, last_face = 2 - 2 * SWEEPS, rows + 2 * SWEEPS - 2
    for chunk in range(size // width):
        there = slice(chunk * width, (chunk + 1) * width)
        inner = slice(PAD + chunk * width, PAD + (chunk + 1) * width)

        def merid_at(row):
            ref, at = row_of(halo_merid, own_merid, row)
            return ref[at, there]

        weights = []
        for face in range(first_face, last_face + 1):
            place = band * rows + face
            open_face = jnp.logical_and(place >= 1, place <= total - 1).astype(F32)
            courant = 0.5 * (merid_at(face - 1) + merid_at(face)) * open_face
            weights.append((courant, slope_weight(courant)))
            if 0 <= face <= rows:
                merid_ref[face, 0, there], merid_ref[face, 1, there] = weights[-1]
        f = []
        for row in range(-rows, 2 * rows):
            ref, at = row_of(f_ref, own_ref, row)
            f.append(ref[at, there if ref is own_ref else inner])
        for at, value in enumerate(lat_step(f, weights)):
            next_ref[at, inner] = value

    swept = rows + 2 * SWEEPS
    for at in range(swept):
        next_ref[at, PAD - 1 : PAD] = next_ref[at, PAD + size - 1 : PAD + size]
        next_ref[at, PAD + size : PAD + size + 1] = next_ref[at, PAD : PAD + 1]
        ref, there = row_of(halo_zonal, own_zonal, at - 2)
        f_ref[at, PAD : PAD + size] = lon_step(
            next_ref, slope_ref, flux_ref, at, ref[there, 0], ref[there, 1]
        )
    for chunk in range(size // width):
        there = slice(chunk * width, (chunk + 1) * width)
        inner = slice(PAD + chunk * width, PAD + (chunk + 1) * width)
        f = [f_ref[at, inner] for at in range(swept)]
        weights = [
            (merid_ref[face, 0, there], merid_ref[face, 1, there]) for face in range(rows + 1)
        ]
        for row, value in enumerate(lat_step(f, weights)):
            out_ref[chunk, row * width : (row + 1) * width] = value


def spread_kernel(sizes, in_ref, out_ref):
    species, levels, rows, parts, width = sizes
    per_part = LANES // width
    for row in range(rows):
        for k in range(parts):
            found = [
                in_ref[k * per_part + j, row * width : (row + 1) * width] for j in range(per_part)
            ]
            out_ref[pl.ds(row * parts + k, species * levels, rows * parts), :] = jnp.concatenate(
                found, axis=0
            ).T


def paired(groups, ref, place):
    rows, width, all_levels = ref.shape
    by_level = ref[...].reshape(rows * width, all_levels).T
    levels = all_levels // groups
    for pair in range(groups // 2):
        for parity in range(2):
            start = (2 * pair + parity) * levels
            lane = parity * rows * width
            place[pair * levels : (pair + 1) * levels, lane : lane + rows * width] = by_level[
                start : start + levels
            ]


def pack_kernel(tracer_ref, wind_ref, out_ref, sems):
    size = tracer_ref.shape[0]
    copies = [
        pltpu.make_async_copy(tracer_ref, out_ref.at[:size], sems.at[0]),
        pltpu.make_async_copy(wind_ref, out_ref.at[size:], sems.at[1]),
    ]
    for copy in copies:
        copy.start()
    for copy in copies:
        copy.wait()


def early_kernel(sizes, groups, *refs):
    sent_ref, inputs, refs = refs[0], refs[1:9], refs[9:]
    outputs, refs = refs[:8], refs[8:]
    places, sems = refs[:8], refs[8]
    own_scratch, prepare_scratch = refs[9:13], refs[13:]
    copies = [
        pltpu.make_async_copy(source, place, sems.at[i])
        for i, (source, place) in enumerate(zip(inputs, places, strict=True))
    ]
    for copy in copies:
        copy.start()
    own_rows(sizes, sent_ref, *outputs[:3], *own_scratch)
    for copy in copies:
        copy.wait()
    prepare(groups, *places, *outputs[3:], *prepare_scratch)


def prepare(
    groups,
    depth_ref,
    share_ref,
    kelvin_ref,
    active_ref,
    factor_ref,
    barrier_ref,
    yield_ref,
    pair_ref,
    overlap_out,
    rate_out,
    active_out,
    pick_out,
    yield_out,
    depth_at,
    kelvin_at,
    lower_at,
):
    rows, width, all_levels = depth_ref.shape
    levels = all_levels // groups
    half = LANES // 2
    odd = lax.broadcasted_iota(jnp.int32, (1, LANES), 1) >= half
    species, reactions = yield_ref.shape

    paired(groups, kelvin_ref, kelvin_at)
    paired(groups, depth_ref, depth_at)
    for parity in range(2):
        for row in range(rows):
            lane = (parity * rows + row) * width
            active_out[:, lane : lane + width] = active_ref[:, row, :]

    def column(ref):
        return jnp.broadcast_to(ref[...], (LANES, ref.shape[1])).T

    base = jnp.zeros((1, LANES), F32)
    for pair in range(groups // 2):
        inside = jnp.zeros((1, LANES), F32)
        for level in range(levels):
            at = pair * levels + level
            lower_at[at : at + 1] = inside
            inside = inside + depth_at[at : at + 1]
        other = pltpu.roll(inside, half, 1)
        start = base + jnp.where(odd, other, 0.0)
        here = slice(pair * levels, (pair + 1) * levels)
        lower_at[here] = lower_at[here] + start
        base = base + (inside + other)
    total = base
    lower = lower_at[...]
    upper = lower + depth_at[...]

    share = column(share_ref)
    share_sum = share[0:1]
    for t in range(1, all_levels):
        share_sum = share_sum + share[t : t + 1]
    below = jnp.zeros((1, LANES), F32)
    target_low = below
    for t in range(all_levels):
        below = below + share[t : t + 1]
        target_top = below / share_sum * total
        shared = jnp.maximum(
            jnp.minimum(upper, target_top) - jnp.maximum(lower, target_low), 0.0
        )
        overlap_out[t] = shared / (share[t : t + 1] / share_sum * total)
        target_low = target_top

    factor, barrier = column(factor_ref), column(barrier_ref)
    for at in range(kelvin_at.shape[0]):
        warmth = 300.0 / kelvin_at[at : at + 1] - 1.0
        rate_out[:, at * LANES : (at + 1) * LANES] = factor * jnp.exp(-barrier * warmth)

    one_species = lax.broadcasted_iota(jnp.int32, (2 * species, reactions), 0) % species
    for which in range(2):
        hit = (one_species == pair_ref[which : which + 1, :]).astype(F32)
        pick_out[which * reactions : (which + 1) * reactions] = hit.T.astype(jnp.bfloat16)
    yields = yield_ref[...].astype(F32).astype(jnp.bfloat16)
    yield_out[:, :reactions] = yields
    yield_out[:, reactions:] = yields


def in_two_parts(value):
    high = value.astype(jnp.bfloat16)
    low = (value - high.astype(F32)).astype(jnp.bfloat16)
    return jnp.concatenate([high, low], axis=0)


def column_kernel(
    sizes,
    moved_ref,
    overlap_ref,
    rate_ref,
    active_ref,
    pick_ref,
    yield_ref,
    out_ref,
    source_ref,
    target_ref,
):
    groups, levels, species, tile_pairs = sizes
    half = LANES // 2
    pairs = groups // 2 * levels
    reactions = yield_ref.shape[1] // 2
    odd = lax.broadcasted_iota(jnp.int32, (1, LANES), 1) >= half

    for pair in range(groups // 2):
        both = jnp.concatenate([moved_ref[2 * pair], moved_ref[2 * pair + 1]], axis=0)
        source_ref[pair] = both.T

    def remapped(at):
        pair, level = divmod(at, levels)
        sums = []
        for parity in range(2):
            t = (2 * pair + parity) * levels + level
            acc = None
            for s in range(pairs):
                source = source_ref[s // levels, pl.ds(s % levels, species, levels), :]
                term = overlap_ref[t, s : s + 1, :] * source
                acc = term if acc is None else acc + term
            sums.append(acc)
        kept = jnp.where(odd, sums[1], sums[0])
        crossed = jnp.where(odd, sums[0], sums[1])
        return kept + pltpu.roll(crossed, half, 1)

    tiles = [range(first, first + tile_pairs) for first in range(0, pairs, tile_pairs)]
    q = [jnp.concatenate([remapped(at) for at in tile], axis=1) for tile in tiles]
    for substep in range(active_ref.shape[0]):
        on = jnp.concatenate([active_ref[substep : substep + 1, :]] * tile_pairs, axis=1) > 0
        picked = [
            jnp.dot(pick_ref[...], in_two_parts(value), preferred_element_type=F32) for value in q
        ]
        rates = [
            rate_ref[:, tile[0] * LANES : (tile[-1] + 1) * LANES]
            * found[:reactions]
            * found[reactions:]
            for tile, found in zip(tiles, picked, strict=True)
        ]
        rates = [in_two_parts(value) for value in rates]
        changes = [
            jnp.dot(yield_ref[...], value, preferred_element_type=F32) for value in rates
        ]
        q = [
            jnp.where(on, value + change, value) for value, change in zip(q, changes, strict=True)
        ]
    for tile, value in zip(tiles, q, strict=True):
        for inside, at in enumerate(tile):
            pair, level = divmod(at, levels)
            lane = inside * LANES
            target_ref[pair, pl.ds(level, species, levels), :] = value[:, lane : lane + LANES]

    for pair in range(groups // 2):
        both = target_ref[pair].T
        out_ref[2 * pair], out_ref[2 * pair + 1] = both[:half], both[half:]


def swap_pairs(count, first):
    route = []
    for low in range(first, count - 1, 2):
        route += [(low, low + 1), (low + 1, low)]
    return route


def kernel_call(kernel, name, outs, scratch, cost=None):
    return pl.pallas_call(
        kernel,
        out_shape=outs,
        scratch_shapes=[pltpu.VMEM(shape, F32) for shape in scratch],
        compiler_params=PARAMS,
        cost_estimate=cost,
        name=name,
    )


def body(
    species_fractions,
    cell_flow_ratios,
    layer_pressure_depth,
    layer_thickness_fraction,
    cell_kelvin_field,
    daytime_indicator,
    kinetic_factor_times_step,
    arrhenius_barrier,
    species_yield_matrix,
    reagent_pairs,
):
    species, levels, rows, lons = species_fractions.shape
    all_levels = layer_pressure_depth.shape[0]
    width = layer_pressure_depth.shape[2]
    blocks = lax.axis_size("lev")
    bands = lax.axis_size("lat")
    parts = lons // LANES
    substeps = daytime_indicator.shape[0]
    reactions = kinetic_factor_times_step.shape[0]
    assert 2 * rows * width == LANES and rows == 2 * SWEEPS and blocks % 2 == 0
    sizes = (species, levels, rows, parts, width)
    mixed = species * levels

    by_core, by_chip = swap_pairs(bands, 0), swap_pairs(bands, 1)
    def flat(value):
        return value.reshape(-1, LANES)

    def in_hbm(*values):
        return [pltpu.with_memory_space_constraint(item, pltpu.HBM) for item in values]

    tracers, winds = flat(species_fractions), flat(cell_flow_ratios)
    sent = pl.pallas_call(
        pack_kernel,
        out_shape=jax.ShapeDtypeStruct((len(tracers) + len(winds), LANES), F32),
        in_specs=[pl.BlockSpec(memory_space=pltpu.HBM)] * 2,
        scratch_shapes=[pltpu.SemaphoreType.DMA((2,))],
        compiler_params=PARAMS,
        name="pack",
    )(*in_hbm(tracers, winds))
    core_band = lax.ppermute(sent, "lat", by_core)
    chip_band = lax.ppermute(sent, "lat", by_chip)

    def arrays(*shapes):
        return [jax.ShapeDtypeStruct(shape, F32) for shape in shapes]

    padded = lons + 2 * PAD
    pairs = all_levels // 2
    operands = (
        layer_pressure_depth.transpose(1, 2, 0),
        layer_thickness_fraction[None],
        cell_kelvin_field.transpose(1, 2, 0),
        daytime_indicator,
        kinetic_factor_times_step[None],
        arrhenius_barrier[None],
        species_yield_matrix.T,
        reagent_pairs,
    )
    early = pl.pallas_call(
        functools.partial(early_kernel, sizes, blocks),
        out_shape=[
            *arrays((rows, lons, mixed), (rows, 2, lons, mixed), (rows, lons, mixed)),
            *arrays((all_levels, pairs, LANES), (reactions, pairs * LANES)),
            jax.ShapeDtypeStruct((substeps, LANES), jnp.int32),
            jax.ShapeDtypeStruct((2 * reactions, 2 * species), jnp.bfloat16),
            jax.ShapeDtypeStruct((species, 2 * reactions), jnp.bfloat16),
        ],
        in_specs=[pl.BlockSpec(memory_space=pltpu.VMEM)]
        + [pl.BlockSpec(memory_space=pltpu.HBM)] * len(operands),
        scratch_shapes=[
            *[pltpu.VMEM(item.shape, item.dtype) for item in operands],
            pltpu.SemaphoreType.DMA((len(operands),)),
            *[pltpu.VMEM((rows, padded, mixed), F32)] * 4,
            *[pltpu.VMEM((pairs, LANES), F32)] * 3,
        ],
        compiler_params=PARAMS,
        cost_estimate=pl.CostEstimate(
            flops=10**7, bytes_accessed=7 * 10**6, transcendentals=10**6
        ),
        name="early",
    )(sent, *in_hbm(*operands))
    own, prepared = early[:3], early[3:]

    packed = kernel_call(
        functools.partial(advect_kernel, sizes),
        "advect",
        arrays((blocks, rows * width, mixed))[0],
        [(2 * rows, padded, mixed)] * 4
        + [
            (2 * rows, 2, lons, mixed),
            (2 * rows, lons, mixed),
            (rows + 1, 2, lons, mixed),
            (2 * rows, padded, mixed),
        ],
    )(*own, chip_band, core_band)
    moved = lax.all_to_all(packed, "lev", split_axis=0, concat_axis=0, tiled=True)

    reacted = kernel_call(
        functools.partial(column_kernel, (blocks, levels, species, pairs // 4)),
        "columns",
        arrays(packed.shape)[0],
        [(blocks // 2, mixed, LANES)] * 2,
    )(moved, *prepared)
    returned = lax.all_to_all(reacted, "lev", split_axis=0, concat_axis=0, tiled=True)
    out = kernel_call(
        functools.partial(spread_kernel, sizes),
        "spread",
        arrays((mixed * rows * parts, LANES))[0],
        [],
    )(returned)
    return out.reshape(species_fractions.shape)


def solution(mesh):
    placed = (
        P(None, "lev", "lat", None),
        P(None, "lev", "lat", None),
        P(None, "lat", "lev"),
        P(),
        P(None, "lat", "lev"),
        P(None, "lat", "lev"),
        P(),
        P(),
        P(),
        P(),
    )
    return jax.shard_map(
        body, mesh=mesh, in_specs=placed, out_specs=P(None, "lev", "lat", None), check_vma=False
    )
```

```python
import functools

import jax
import jax.numpy as jnp
from jax import lax
from jax.experimental import pallas as pl
from jax.experimental.pallas import tpu as pltpu
from jax.sharding import PartitionSpec as P

LANES = 128
PAD = 8
SWEEPS = 2
PARAMS = pltpu.CompilerParams(vmem_limit_bytes=16 * 2**20)
F32 = jnp.float32


def limited_slope(left, right):
    return jnp.maximum(jnp.minimum(left, right), 0.0) + jnp.minimum(jnp.maximum(left, right), 0.0)


def slope_weight(courant):
    return courant * (0.5 * (jnp.where(courant > 0.0, 1.0, -1.0) - courant))


def face_flux(courant, weight, before, after, before_slope, after_slope):
    ahead = courant > 0.0
    return courant * jnp.where(ahead, before, after) + weight * jnp.where(
        ahead, before_slope, after_slope
    )


def put_cyclic(ref, row, value):
    size = value.shape[0]
    ref[row, PAD : PAD + size] = value
    ref[row, PAD - 1 : PAD] = value[size - 1 :]
    ref[row, PAD + size : PAD + size + 1] = value[:1]


def shifted(ref, row, size, by):
    return ref[row, PAD + by : PAD + by + size]


def lon_step(f_ref, slope_ref, flux_ref, row, courant, weight):
    size = courant.shape[0]
    f, left, right = (shifted(f_ref, row, size, by) for by in (0, -1, 1))
    slope = limited_slope(f - left, right - f)
    put_cyclic(slope_ref, row, slope)
    flux = face_flux(courant, weight, left, f, shifted(slope_ref, row, size, -1), slope)
    put_cyclic(flux_ref, row, flux)
    return f - (shifted(flux_ref, row, size, 1) - flux)


def lat_step(f, weights):
    jumps = [f[i + 1] - f[i] for i in range(len(f) - 1)]
    slopes = [None] + [limited_slope(jumps[i - 1], jumps[i]) for i in range(1, len(f) - 1)]
    fluxes = [
        face_flux(*weights[i - 2], f[i - 1], f[i], slopes[i - 1], slopes[i])
        for i in range(2, len(f) - 1)
    ]
    return [f[i] - (fluxes[i - 1] - fluxes[i - 2]) for i in range(2, len(f) - 2)]


def tracer_rows(sizes, ref, row):
    species, levels, rows, parts, _ = sizes
    return [
        ref[pl.ds(row * parts + k, species * levels, rows * parts), :] for k in range(parts)
    ]


def flow_rows(sizes, ref, which, row, skip=0):
    species, levels, rows, parts, _ = sizes
    found = []
    for k in range(parts):
        start = ((skip + which) * levels * rows + row) * parts + k
        level_rows = ref[pl.ds(start, levels, rows * parts), :]
        tile = jnp.concatenate([level_rows] * (8 // levels), axis=0)
        found.append(jnp.concatenate([tile] * (species * levels // 8), axis=0))
    return found


def turned(tiles):
    return jnp.concatenate([tile.T for tile in tiles], axis=0)


def zonal_weights(flow_ref, row, flow):
    put_cyclic(flow_ref, row, flow)
    courant = 0.5 * (shifted(flow_ref, row, flow.shape[0], -1) + flow)
    return courant, slope_weight(courant)


def near_rows(
    sizes, sent_ref, core_ref, f_out, zonal_out, merid_out, f_ref, slope_ref, flux_ref, flow_ref
):
    rows = sizes[2]
    for side, source in enumerate((sent_ref, core_ref)):
        for row in range(rows):
            at = side * rows + row
            first_sweep(
                sizes, source, row, at, at, f_out, zonal_out, merid_out, f_ref, slope_ref, flux_ref, flow_ref
            )


def first_sweep(
    sizes, source, row, at, to, f_out, zonal_out, merid_out, f_ref, slope_ref, flux_ref, flow_ref, skip=0
):
    species = sizes[0]
    courant, weight = zonal_weights(
        flow_ref, at, turned(flow_rows(sizes, source, 0, row, species))
    )
    zonal_out[to, 0], zonal_out[to, 1] = courant, weight
    merid_out[to] = turned(flow_rows(sizes, source, 1, row, species))
    put_cyclic(f_ref, at, turned(tracer_rows(sizes, source, row)))
    f_out[to, skip : skip + courant.shape[0]] = lon_step(
        f_ref, slope_ref, flux_ref, at, courant, weight
    )


def advect_kernel(
    sizes,
    own_ref,
    own_zonal,
    own_merid,
    chip_ref,
    out_ref,
    f_ref,
    slope_ref,
    flux_ref,
    flow_ref,
    halo_zonal,
    halo_merid,
    merid_ref,
    next_ref,
):
    species, levels, rows, parts, width = sizes
    band = lax.axis_index("lat")
    size = own_ref.shape[1]
    chip_at = (band % 2) * rows
    core_at = rows - chip_at
    for row in range(rows):
        first_sweep(
            sizes,
            chip_ref,
            row,
            row,
            chip_at + row,
            f_ref,
            halo_zonal,
            halo_merid,
            next_ref,
            slope_ref,
            flux_ref,
            flow_ref,
            PAD,
        )
        f_ref[core_at + row, PAD : PAD + size] = own_ref[rows + row]
        halo_zonal[core_at + row] = own_zonal[rows + row]
        halo_merid[core_at + row] = own_merid[rows + row]

    def row_of(halo, own, row):
        if 0 <= row < rows:
            return own, row
        return halo, (row + rows if row < 0 else row)

    total = rows * lax.axis_size("lat")
    first_face, last_face = 2 - 2 * SWEEPS, rows + 2 * SWEEPS - 2
    for chunk in range(size // width):
        there = slice(chunk * width, (chunk + 1) * width)
        inner = slice(PAD + chunk * width, PAD + (chunk + 1) * width)

        def merid_at(row):
            ref, at = row_of(halo_merid, own_merid, row)
            return ref[at, there]

        weights = []
        for face in range(first_face, last_face + 1):
            place = band * rows + face
            open_face = jnp.logical_and(place >= 1, place <= total - 1).astype(F32)
            courant = 0.5 * (merid_at(face - 1) + merid_at(face)) * open_face
            weights.append((courant, slope_weight(courant)))
            if 0 <= face <= rows:
                merid_ref[face, 0, there], merid_ref[face, 1, there] = weights[-1]
        f = []
        for row in range(-rows, 2 * rows):
            ref, at = row_of(f_ref, own_ref, row)
            f.append(ref[at, there if ref is own_ref else inner])
        for at, value in enumerate(lat_step(f, weights)):
            next_ref[at, inner] = value

    swept = rows + 2 * SWEEPS
    for at in range(swept):
        next_ref[at, PAD - 1 : PAD] = next_ref[at, PAD + size - 1 : PAD + size]
        next_ref[at, PAD + size : PAD + size + 1] = next_ref[at, PAD : PAD + 1]
        ref, there = row_of(halo_zonal, own_zonal, at - 2)
        f_ref[at, PAD : PAD + size] = lon_step(
            next_ref, slope_ref, flux_ref, at, ref[there, 0], ref[there, 1]
        )
    for chunk in range(size // width):
        there = slice(chunk * width, (chunk + 1) * width)
        inner = slice(PAD + chunk * width, PAD + (chunk + 1) * width)
        f = [f_ref[at, inner] for at in range(swept)]
        weights = [
            (merid_ref[face, 0, there], merid_ref[face, 1, there]) for face in range(rows + 1)
        ]
        for row, value in enumerate(lat_step(f, weights)):
            out_ref[chunk, row * width : (row + 1) * width] = value


def spread_kernel(sizes, in_ref, out_ref):
    species, levels, rows, parts, width = sizes
    per_part = LANES // width
    for row in range(rows):
        for k in range(parts):
            found = [
                in_ref[k * per_part + j, row * width : (row + 1) * width] for j in range(per_part)
            ]
            out_ref[pl.ds(row * parts + k, species * levels, rows * parts), :] = jnp.concatenate(
                found, axis=0
            ).T


def paired(groups, ref, place):
    rows, width, all_levels = ref.shape
    by_level = ref[...].reshape(rows * width, all_levels).T
    levels = all_levels // groups
    for pair in range(groups // 2):
        for parity in range(2):
            start = (2 * pair + parity) * levels
            lane = parity * rows * width
            place[pair * levels : (pair + 1) * levels, lane : lane + rows * width] = by_level[
                start : start + levels
            ]


def pack_kernel(tracer_ref, wind_ref, out_ref, sems):
    size = tracer_ref.shape[0]
    copies = [
        pltpu.make_async_copy(tracer_ref, out_ref.at[:size], sems.at[0]),
        pltpu.make_async_copy(wind_ref, out_ref.at[size:], sems.at[1]),
    ]
    for copy in copies:
        copy.start()
    for copy in copies:
        copy.wait()


def early_kernel(sizes, groups, *refs):
    sent_ref, core_ref, inputs, refs = refs[0], refs[1], refs[2:10], refs[10:]
    outputs, refs = refs[:8], refs[8:]
    places, sems = refs[:8], refs[8]
    own_scratch, prepare_scratch = refs[9:13], refs[13:]
    copies = [
        pltpu.make_async_copy(source, place, sems.at[i])
        for i, (source, place) in enumerate(zip(inputs, places, strict=True))
    ]
    for copy in copies:
        copy.start()
    near_rows(sizes, sent_ref, core_ref, *outputs[:3], *own_scratch)
    for copy in copies:
        copy.wait()
    prepare(groups, *places, *outputs[3:], *prepare_scratch)


def prepare(
    groups,
    depth_ref,
    share_ref,
    kelvin_ref,
    active_ref,
    factor_ref,
    barrier_ref,
    yield_ref,
    pair_ref,
    overlap_out,
    rate_out,
    active_out,
    pick_out,
    yield_out,
    depth_at,
    kelvin_at,
    lower_at,
):
    rows, width, all_levels = depth_ref.shape
    levels = all_levels // groups
    half = LANES // 2
    odd = lax.broadcasted_iota(jnp.int32, (1, LANES), 1) >= half
    species, reactions = yield_ref.shape

    paired(groups, kelvin_ref, kelvin_at)
    paired(groups, depth_ref, depth_at)
    for parity in range(2):
        for row in range(rows):
            lane = (parity * rows + row) * width
            active_out[:, lane : lane + width] = active_ref[:, row, :]

    def column(ref):
        return jnp.broadcast_to(ref[...], (LANES, ref.shape[1])).T

    base = jnp.zeros((1, LANES), F32)
    for pair in range(groups // 2):
        inside = jnp.zeros((1, LANES), F32)
        for level in range(levels):
            at = pair * levels + level
            lower_at[at : at + 1] = inside
            inside = inside + depth_at[at : at + 1]
        other = pltpu.roll(inside, half, 1)
        start = base + jnp.where(odd, other, 0.0)
        here = slice(pair * levels, (pair + 1) * levels)
        lower_at[here] = lower_at[here] + start
        base = base + (inside + other)
    total = base
    lower = lower_at[...]
    upper = lower + depth_at[...]

    share = column(share_ref)
    share_sum = share[0:1]
    for t in range(1, all_levels):
        share_sum = share_sum + share[t : t + 1]
    below = jnp.zeros((1, LANES), F32)
    target_low = below
    for t in range(all_levels):
        below = below + share[t : t + 1]
        target_top = below / share_sum * total
        shared = jnp.maximum(
            jnp.minimum(upper, target_top) - jnp.maximum(lower, target_low), 0.0
        )
        overlap_out[t] = shared / (share[t : t + 1] / share_sum * total)
        target_low = target_top

    factor, barrier = column(factor_ref), column(barrier_ref)
    for at in range(kelvin_at.shape[0]):
        warmth = 300.0 / kelvin_at[at : at + 1] - 1.0
        rate_out[:, at * LANES : (at + 1) * LANES] = factor * jnp.exp(-barrier * warmth)

    one_species = lax.broadcasted_iota(jnp.int32, (2 * species, reactions), 0) % species
    for which in range(2):
        hit = (one_species == pair_ref[which : which + 1, :]).astype(F32)
        pick_out[which * reactions : (which + 1) * reactions] = hit.T.astype(jnp.bfloat16)
    yields = yield_ref[...].astype(F32).astype(jnp.bfloat16)
    yield_out[:, :reactions] = yields
    yield_out[:, reactions:] = yields


def in_two_parts(value):
    high = value.astype(jnp.bfloat16)
    low = (value - high.astype(F32)).astype(jnp.bfloat16)
    return jnp.concatenate([high, low], axis=0)


def column_kernel(
    sizes,
    moved_ref,
    overlap_ref,
    rate_ref,
    active_ref,
    pick_ref,
    yield_ref,
    out_ref,
    source_ref,
    target_ref,
):
    groups, levels, species, tile_pairs = sizes
    half = LANES // 2
    pairs = groups // 2 * levels
    reactions = yield_ref.shape[1] // 2
    odd = lax.broadcasted_iota(jnp.int32, (1, LANES), 1) >= half

    for pair in range(groups // 2):
        both = jnp.concatenate([moved_ref[2 * pair], moved_ref[2 * pair + 1]], axis=0)
        source_ref[pair] = both.T

    def remapped(at):
        pair, level = divmod(at, levels)
        sums = []
        for parity in range(2):
            t = (2 * pair + parity) * levels + level
            acc = None
            for s in range(pairs):
                source = source_ref[s // levels, pl.ds(s % levels, species, levels), :]
                term = overlap_ref[t, s : s + 1, :] * source
                acc = term if acc is None else acc + term
            sums.append(acc)
        kept = jnp.where(odd, sums[1], sums[0])
        crossed = jnp.where(odd, sums[0], sums[1])
        return kept + pltpu.roll(crossed, half, 1)

    tiles = [range(first, first + tile_pairs) for first in range(0, pairs, tile_pairs)]
    q = [jnp.concatenate([remapped(at) for at in tile], axis=1) for tile in tiles]
    for substep in range(active_ref.shape[0]):
        on = jnp.concatenate([active_ref[substep : substep + 1, :]] * tile_pairs, axis=1) > 0
        picked = [
            jnp.dot(pick_ref[...], in_two_parts(value), preferred_element_type=F32) for value in q
        ]
        rates = [
            rate_ref[:, tile[0] * LANES : (tile[-1] + 1) * LANES]
            * found[:reactions]
            * found[reactions:]
            for tile, found in zip(tiles, picked, strict=True)
        ]
        rates = [in_two_parts(value) for value in rates]
        changes = [
            jnp.dot(yield_ref[...], value, preferred_element_type=F32) for value in rates
        ]
        q = [
            jnp.where(on, value + change, value) for value, change in zip(q, changes, strict=True)
        ]
    for tile, value in zip(tiles, q, strict=True):
        for inside, at in enumerate(tile):
            pair, level = divmod(at, levels)
            lane = inside * LANES
            target_ref[pair, pl.ds(level, species, levels), :] = value[:, lane : lane + LANES]

    for pair in range(groups // 2):
        both = target_ref[pair].T
        out_ref[2 * pair], out_ref[2 * pair + 1] = both[:half], both[half:]


def swap_pairs(count, first):
    route = []
    for low in range(first, count - 1, 2):
        route += [(low, low + 1), (low + 1, low)]
    return route


def kernel_call(kernel, name, outs, scratch, cost=None):
    return pl.pallas_call(
        kernel,
        out_shape=outs,
        scratch_shapes=[pltpu.VMEM(shape, F32) for shape in scratch],
        compiler_params=PARAMS,
        cost_estimate=cost,
        name=name,
    )


def body(
    species_fractions,
    cell_flow_ratios,
    layer_pressure_depth,
    layer_thickness_fraction,
    cell_kelvin_field,
    daytime_indicator,
    kinetic_factor_times_step,
    arrhenius_barrier,
    species_yield_matrix,
    reagent_pairs,
):
    species, levels, rows, lons = species_fractions.shape
    all_levels = layer_pressure_depth.shape[0]
    width = layer_pressure_depth.shape[2]
    blocks = lax.axis_size("lev")
    bands = lax.axis_size("lat")
    parts = lons // LANES
    substeps = daytime_indicator.shape[0]
    reactions = kinetic_factor_times_step.shape[0]
    assert 2 * rows * width == LANES and rows == 2 * SWEEPS and blocks % 2 == 0
    sizes = (species, levels, rows, parts, width)
    mixed = species * levels

    by_core, by_chip = swap_pairs(bands, 0), swap_pairs(bands, 1)
    def flat(value):
        return value.reshape(-1, LANES)

    def in_hbm(*values):
        return [pltpu.with_memory_space_constraint(item, pltpu.HBM) for item in values]

    tracers, winds = flat(species_fractions), flat(cell_flow_ratios)
    sent = pl.pallas_call(
        pack_kernel,
        out_shape=jax.ShapeDtypeStruct((len(tracers) + len(winds), LANES), F32),
        in_specs=[pl.BlockSpec(memory_space=pltpu.HBM)] * 2,
        scratch_shapes=[pltpu.SemaphoreType.DMA((2,))],
        compiler_params=PARAMS,
        name="pack",
    )(*in_hbm(tracers, winds))
    core_band = lax.ppermute(sent, "lat", by_core)
    chip_band = lax.ppermute(sent, "lat", by_chip)

    def arrays(*shapes):
        return [jax.ShapeDtypeStruct(shape, F32) for shape in shapes]

    padded = lons + 2 * PAD
    pairs = all_levels // 2
    operands = (
        layer_pressure_depth.transpose(1, 2, 0),
        layer_thickness_fraction[None],
        cell_kelvin_field.transpose(1, 2, 0),
        daytime_indicator,
        kinetic_factor_times_step[None],
        arrhenius_barrier[None],
        species_yield_matrix.T,
        reagent_pairs,
    )
    early = pl.pallas_call(
        functools.partial(early_kernel, sizes, blocks),
        out_shape=[
            *arrays((2 * rows, lons, mixed), (2 * rows, 2, lons, mixed), (2 * rows, lons, mixed)),
            *arrays((all_levels, pairs, LANES), (reactions, pairs * LANES)),
            jax.ShapeDtypeStruct((substeps, LANES), jnp.int32),
            jax.ShapeDtypeStruct((2 * reactions, 2 * species), jnp.bfloat16),
            jax.ShapeDtypeStruct((species, 2 * reactions), jnp.bfloat16),
        ],
        in_specs=[pl.BlockSpec(memory_space=pltpu.VMEM)] * 2
        + [pl.BlockSpec(memory_space=pltpu.HBM)] * len(operands),
        scratch_shapes=[
            *[pltpu.VMEM(item.shape, item.dtype) for item in operands],
            pltpu.SemaphoreType.DMA((len(operands),)),
            *[pltpu.VMEM((2 * rows, padded, mixed), F32)] * 4,
            *[pltpu.VMEM((pairs, LANES), F32)] * 3,
        ],
        compiler_params=PARAMS,
        cost_estimate=pl.CostEstimate(
            flops=10**7, bytes_accessed=7 * 10**6, transcendentals=10**6
        ),
        name="early",
    )(sent, core_band, *in_hbm(*operands))
    near, prepared = early[:3], early[3:]

    packed = kernel_call(
        functools.partial(advect_kernel, sizes),
        "advect",
        arrays((blocks, rows * width, mixed))[0],
        [(2 * rows, padded, mixed)] * 4
        + [
            (2 * rows, 2, lons, mixed),
            (2 * rows, lons, mixed),
            (rows + 1, 2, lons, mixed),
            (2 * rows, padded, mixed),
        ],
    )(*near, chip_band)
    moved = lax.all_to_all(packed, "lev", split_axis=0, concat_axis=0, tiled=True)

    reacted = kernel_call(
        functools.partial(column_kernel, (blocks, levels, species, pairs // 4)),
        "columns",
        arrays(packed.shape)[0],
        [(blocks // 2, mixed, LANES)] * 2,
    )(moved, *prepared)
    returned = lax.all_to_all(reacted, "lev", split_axis=0, concat_axis=0, tiled=True)
    out = kernel_call(
        functools.partial(spread_kernel, sizes),
        "spread",
        arrays((mixed * rows * parts, LANES))[0],
        [],
    )(returned)
    return out.reshape(species_fractions.shape)


def solution(mesh):
    placed = (
        P(None, "lev", "lat", None),
        P(None, "lev", "lat", None),
        P(None, "lat", "lev"),
        P(),
        P(None, "lat", "lev"),
        P(None, "lat", "lev"),
        P(),
        P(),
        P(),
        P(),
    )
    return jax.shard_map(
        body, mesh=mesh, in_specs=placed, out_specs=P(None, "lev", "lat", None), check_vma=False
    )
```

```python
import functools

import jax
import jax.numpy as jnp
from jax import lax
from jax.experimental import pallas as pl
from jax.experimental.pallas import tpu as pltpu
from jax.sharding import PartitionSpec as P

LANES = 128
PAD = 8
SWEEPS = 2
PARAMS = pltpu.CompilerParams(vmem_limit_bytes=16 * 2**20)
F32 = jnp.float32


def limited_slope(left, right):
    return jnp.maximum(jnp.minimum(right, jnp.maximum(left, 0.0)), jnp.minimum(left, 0.0))


def slope_weight(courant):
    return courant * (0.5 * (jnp.where(courant > 0.0, 1.0, -1.0) - courant))


def face_flux(courant, weight, before, after, before_slope, after_slope):
    ahead = courant > 0.0
    return courant * jnp.where(ahead, before, after) + weight * jnp.where(
        ahead, before_slope, after_slope
    )


def put_cyclic(ref, row, value):
    size = value.shape[0]
    ref[row, PAD : PAD + size] = value
    ref[row, PAD - 1 : PAD] = value[size - 1 :]
    ref[row, PAD + size : PAD + size + 1] = value[:1]


def shifted(ref, row, size, by):
    return ref[row, PAD + by : PAD + by + size]


def lon_step(f_ref, slope_ref, flux_ref, row, courant, weight):
    size = courant.shape[0]
    f, left, right = (shifted(f_ref, row, size, by) for by in (0, -1, 1))
    slope = limited_slope(f - left, right - f)
    put_cyclic(slope_ref, row, slope)
    flux = face_flux(courant, weight, left, f, shifted(slope_ref, row, size, -1), slope)
    put_cyclic(flux_ref, row, flux)
    return f - (shifted(flux_ref, row, size, 1) - flux)


def lat_step(f, weights):
    jumps = [f[i + 1] - f[i] for i in range(len(f) - 1)]
    slopes = [None] + [limited_slope(jumps[i - 1], jumps[i]) for i in range(1, len(f) - 1)]
    fluxes = [
        face_flux(*weights[i - 2], f[i - 1], f[i], slopes[i - 1], slopes[i])
        for i in range(2, len(f) - 1)
    ]
    return [f[i] - (fluxes[i - 1] - fluxes[i - 2]) for i in range(2, len(f) - 2)]


def tracer_rows(sizes, ref, row):
    species, levels, rows, parts, _ = sizes
    return [
        ref[pl.ds(row * parts + k, species * levels, rows * parts), :] for k in range(parts)
    ]


def flow_rows(sizes, ref, which, row, skip=0):
    species, levels, rows, parts, _ = sizes
    found = []
    for k in range(parts):
        start = ((skip + which) * levels * rows + row) * parts + k
        level_rows = ref[pl.ds(start, levels, rows * parts), :]
        tile = jnp.concatenate([level_rows] * (8 // levels), axis=0)
        found.append(jnp.concatenate([tile] * (species * levels // 8), axis=0))
    return found


def turned(tiles):
    return jnp.concatenate([tile.T for tile in tiles], axis=0)


def zonal_weights(flow_ref, row, flow):
    put_cyclic(flow_ref, row, flow)
    courant = 0.5 * (shifted(flow_ref, row, flow.shape[0], -1) + flow)
    return courant, slope_weight(courant)


def near_rows(
    sizes, sent_ref, core_ref, f_out, zonal_out, merid_out, f_ref, slope_ref, flux_ref, flow_ref
):
    rows = sizes[2]
    for side, source in enumerate((sent_ref, core_ref)):
        for row in range(rows):
            at = side * rows + row
            first_sweep(
                sizes, source, row, at, at, f_out, zonal_out, merid_out, f_ref, slope_ref, flux_ref, flow_ref
            )


def first_sweep(
    sizes, source, row, at, to, f_out, zonal_out, merid_out, f_ref, slope_ref, flux_ref, flow_ref, skip=0
):
    species = sizes[0]
    courant, weight = zonal_weights(
        flow_ref, at, turned(flow_rows(sizes, source, 0, row, species))
    )
    zonal_out[to, 0], zonal_out[to, 1] = courant, weight
    merid_out[to] = turned(flow_rows(sizes, source, 1, row, species))
    put_cyclic(f_ref, at, turned(tracer_rows(sizes, source, row)))
    f_out[to, skip : skip + courant.shape[0]] = lon_step(
        f_ref, slope_ref, flux_ref, at, courant, weight
    )


def advect_kernel(
    sizes,
    inner_merid,
    own_ref,
    own_zonal,
    own_merid,
    chip_ref,
    out_ref,
    f_ref,
    slope_ref,
    flux_ref,
    flow_ref,
    halo_zonal,
    halo_merid,
    merid_ref,
    next_ref,
):
    species, levels, rows, parts, width = sizes
    band = lax.axis_index("lat")
    size = own_ref.shape[1]
    chip_at = (band % 2) * rows
    core_at = rows - chip_at
    for row in range(rows):
        first_sweep(
            sizes,
            chip_ref,
            row,
            row,
            chip_at + row,
            f_ref,
            halo_zonal,
            halo_merid,
            next_ref,
            slope_ref,
            flux_ref,
            flow_ref,
            PAD,
        )
        f_ref[core_at + row, PAD : PAD + size] = own_ref[rows + row]
        halo_zonal[core_at + row] = own_zonal[rows + row]
        halo_merid[core_at + row] = own_merid[rows + row]

    def row_of(halo, own, row):
        if 0 <= row < rows:
            return own, row
        return halo, (row + rows if row < 0 else row)

    total = rows * lax.axis_size("lat")
    first_face, last_face = 2 - 2 * SWEEPS, rows + 2 * SWEEPS - 2
    for chunk in range(size // width):
        there = slice(chunk * width, (chunk + 1) * width)
        inner = slice(PAD + chunk * width, PAD + (chunk + 1) * width)

        def merid_at(row):
            ref, at = row_of(halo_merid, own_merid, row)
            return ref[at, there]

        weights = []
        for face in range(first_face, last_face + 1):
            if 1 <= face < rows:
                weights.append((inner_merid[face - 1, 0, there], inner_merid[face - 1, 1, there]))
                continue
            place = band * rows + face
            open_face = jnp.logical_and(place >= 1, place <= total - 1).astype(F32)
            courant = 0.5 * (merid_at(face - 1) + merid_at(face)) * open_face
            weights.append((courant, slope_weight(courant)))
            if face in (0, rows):
                at = face // rows
                merid_ref[at, 0, there], merid_ref[at, 1, there] = weights[-1]
        f = []
        for row in range(-rows, 2 * rows):
            ref, at = row_of(f_ref, own_ref, row)
            f.append(ref[at, there if ref is own_ref else inner])
        for at, value in enumerate(lat_step(f, weights)):
            next_ref[at, inner] = value

    swept = rows + 2 * SWEEPS
    for at in range(swept):
        next_ref[at, PAD - 1 : PAD] = next_ref[at, PAD + size - 1 : PAD + size]
        next_ref[at, PAD + size : PAD + size + 1] = next_ref[at, PAD : PAD + 1]
        ref, there = row_of(halo_zonal, own_zonal, at - 2)
        f_ref[at, PAD : PAD + size] = lon_step(
            next_ref, slope_ref, flux_ref, at, ref[there, 0], ref[there, 1]
        )
    for chunk in range(size // width):
        there = slice(chunk * width, (chunk + 1) * width)
        inner = slice(PAD + chunk * width, PAD + (chunk + 1) * width)
        f = [f_ref[at, inner] for at in range(swept)]
        faces = [(merid_ref, 0), *[(inner_merid, at) for at in range(rows - 1)], (merid_ref, 1)]
        weights = [(ref[at, 0, there], ref[at, 1, there]) for ref, at in faces]
        for row, value in enumerate(lat_step(f, weights)):
            out_ref[chunk, row * width : (row + 1) * width] = value


def spread_kernel(sizes, in_ref, out_ref):
    species, levels, rows, parts, width = sizes
    per_part = LANES // width
    for row in range(rows):
        for k in range(parts):
            found = [
                in_ref[k * per_part + j, row * width : (row + 1) * width] for j in range(per_part)
            ]
            out_ref[pl.ds(row * parts + k, species * levels, rows * parts), :] = jnp.concatenate(
                found, axis=0
            ).T


def paired(groups, ref, place):
    rows, width, all_levels = ref.shape
    by_level = ref[...].reshape(rows * width, all_levels).T
    levels = all_levels // groups
    for pair in range(groups // 2):
        for parity in range(2):
            start = (2 * pair + parity) * levels
            lane = parity * rows * width
            place[pair * levels : (pair + 1) * levels, lane : lane + rows * width] = by_level[
                start : start + levels
            ]


def pack_kernel(tracer_ref, wind_ref, out_ref, sems):
    size = tracer_ref.shape[0]
    copies = [
        pltpu.make_async_copy(tracer_ref, out_ref.at[:size], sems.at[0]),
        pltpu.make_async_copy(wind_ref, out_ref.at[size:], sems.at[1]),
    ]
    for copy in copies:
        copy.start()
    for copy in copies:
        copy.wait()


def early_kernel(sizes, groups, *refs):
    sent_ref, core_ref, inputs, refs = refs[0], refs[1], refs[2:10], refs[10:]
    inner_out, refs = refs[0], refs[1:]
    outputs, refs = refs[:8], refs[8:]
    places, sems = refs[:8], refs[8]
    own_scratch, prepare_scratch = refs[9:13], refs[13:]
    copies = [
        pltpu.make_async_copy(source, place, sems.at[i])
        for i, (source, place) in enumerate(zip(inputs, places, strict=True))
    ]
    for copy in copies:
        copy.start()
    near_rows(sizes, sent_ref, core_ref, *outputs[:3], *own_scratch)
    merid = outputs[2]
    for face in range(1, sizes[2]):
        courant = 0.5 * (merid[face - 1] + merid[face])
        inner_out[face - 1, 0], inner_out[face - 1, 1] = courant, slope_weight(courant)
    for copy in copies:
        copy.wait()
    prepare(groups, *places, *outputs[3:], *prepare_scratch)


def prepare(
    groups,
    depth_ref,
    share_ref,
    kelvin_ref,
    active_ref,
    factor_ref,
    barrier_ref,
    yield_ref,
    pair_ref,
    overlap_out,
    rate_out,
    active_out,
    pick_out,
    yield_out,
    depth_at,
    kelvin_at,
    lower_at,
):
    rows, width, all_levels = depth_ref.shape
    levels = all_levels // groups
    half = LANES // 2
    odd = lax.broadcasted_iota(jnp.int32, (1, LANES), 1) >= half
    species, reactions = yield_ref.shape

    paired(groups, kelvin_ref, kelvin_at)
    paired(groups, depth_ref, depth_at)
    for parity in range(2):
        for row in range(rows):
            lane = (parity * rows + row) * width
            active_out[:, lane : lane + width] = active_ref[:, row, :]

    def column(ref):
        return jnp.broadcast_to(ref[...], (LANES, ref.shape[1])).T

    base = jnp.zeros((1, LANES), F32)
    for pair in range(groups // 2):
        inside = jnp.zeros((1, LANES), F32)
        for level in range(levels):
            at = pair * levels + level
            lower_at[at : at + 1] = inside
            inside = inside + depth_at[at : at + 1]
        other = pltpu.roll(inside, half, 1)
        start = base + jnp.where(odd, other, 0.0)
        here = slice(pair * levels, (pair + 1) * levels)
        lower_at[here] = lower_at[here] + start
        base = base + (inside + other)
    total = base
    lower = lower_at[...]
    upper = lower + depth_at[...]

    share = column(share_ref)
    share_sum = share[0:1]
    for t in range(1, all_levels):
        share_sum = share_sum + share[t : t + 1]
    below = jnp.zeros((1, LANES), F32)
    target_low = below
    for t in range(all_levels):
        below = below + share[t : t + 1]
        target_top = below / share_sum * total
        shared = jnp.maximum(
            jnp.minimum(upper, target_top) - jnp.maximum(lower, target_low), 0.0
        )
        overlap_out[t] = shared / (share[t : t + 1] / share_sum * total)
        target_low = target_top

    factor, barrier = column(factor_ref), column(barrier_ref)
    for at in range(kelvin_at.shape[0]):
        warmth = 300.0 / kelvin_at[at : at + 1] - 1.0
        rate_out[:, at * LANES : (at + 1) * LANES] = factor * jnp.exp(-barrier * warmth)

    one_species = lax.broadcasted_iota(jnp.int32, (2 * species, reactions), 0) % species
    for which in range(2):
        hit = (one_species == pair_ref[which : which + 1, :]).astype(F32)
        pick_out[which * reactions : (which + 1) * reactions] = hit.T.astype(jnp.bfloat16)
    yields = yield_ref[...].astype(F32).astype(jnp.bfloat16)
    yield_out[:, :reactions] = yields
    yield_out[:, reactions:] = yields


def in_two_parts(value):
    high = value.astype(jnp.bfloat16)
    low = (value - high.astype(F32)).astype(jnp.bfloat16)
    return jnp.concatenate([high, low], axis=0)


def column_kernel(
    sizes,
    moved_ref,
    overlap_ref,
    rate_ref,
    active_ref,
    pick_ref,
    yield_ref,
    out_ref,
    source_ref,
    target_ref,
):
    groups, levels, species, tile_pairs = sizes
    half = LANES // 2
    pairs = groups // 2 * levels
    reactions = yield_ref.shape[1] // 2
    odd = lax.broadcasted_iota(jnp.int32, (1, LANES), 1) >= half

    for pair in range(groups // 2):
        both = jnp.concatenate([moved_ref[2 * pair], moved_ref[2 * pair + 1]], axis=0)
        source_ref[pair] = both.T

    def remapped(at):
        pair, level = divmod(at, levels)
        sums = []
        for parity in range(2):
            t = (2 * pair + parity) * levels + level
            acc = None
            for s in range(pairs):
                source = source_ref[s // levels, pl.ds(s % levels, species, levels), :]
                term = overlap_ref[t, s : s + 1, :] * source
                acc = term if acc is None else acc + term
            sums.append(acc)
        kept = jnp.where(odd, sums[1], sums[0])
        crossed = jnp.where(odd, sums[0], sums[1])
        return kept + pltpu.roll(crossed, half, 1)

    tiles = [range(first, first + tile_pairs) for first in range(0, pairs, tile_pairs)]
    q = [jnp.concatenate([remapped(at) for at in tile], axis=1) for tile in tiles]
    for substep in range(active_ref.shape[0]):
        on = jnp.concatenate([active_ref[substep : substep + 1, :]] * tile_pairs, axis=1) > 0
        picked = [
            jnp.dot(pick_ref[...], in_two_parts(value), preferred_element_type=F32) for value in q
        ]
        rates = [
            rate_ref[:, tile[0] * LANES : (tile[-1] + 1) * LANES]
            * found[:reactions]
            * found[reactions:]
            for tile, found in zip(tiles, picked, strict=True)
        ]
        rates = [in_two_parts(value) for value in rates]
        changes = [
            jnp.dot(yield_ref[...], value, preferred_element_type=F32) for value in rates
        ]
        q = [
            jnp.where(on, value + change, value) for value, change in zip(q, changes, strict=True)
        ]
    for tile, value in zip(tiles, q, strict=True):
        for inside, at in enumerate(tile):
            pair, level = divmod(at, levels)
            lane = inside * LANES
            target_ref[pair, pl.ds(level, species, levels), :] = value[:, lane : lane + LANES]

    for pair in range(groups // 2):
        both = target_ref[pair].T
        out_ref[2 * pair], out_ref[2 * pair + 1] = both[:half], both[half:]


def swap_pairs(count, first):
    route = []
    for low in range(first, count - 1, 2):
        route += [(low, low + 1), (low + 1, low)]
    return route


def kernel_call(kernel, name, outs, scratch, cost=None):
    return pl.pallas_call(
        kernel,
        out_shape=outs,
        scratch_shapes=[pltpu.VMEM(shape, F32) for shape in scratch],
        compiler_params=PARAMS,
        cost_estimate=cost,
        name=name,
    )


def body(
    species_fractions,
    cell_flow_ratios,
    layer_pressure_depth,
    layer_thickness_fraction,
    cell_kelvin_field,
    daytime_indicator,
    kinetic_factor_times_step,
    arrhenius_barrier,
    species_yield_matrix,
    reagent_pairs,
):
    species, levels, rows, lons = species_fractions.shape
    all_levels = layer_pressure_depth.shape[0]
    width = layer_pressure_depth.shape[2]
    blocks = lax.axis_size("lev")
    bands = lax.axis_size("lat")
    parts = lons // LANES
    substeps = daytime_indicator.shape[0]
    reactions = kinetic_factor_times_step.shape[0]
    assert 2 * rows * width == LANES and rows == 2 * SWEEPS and blocks % 2 == 0
    sizes = (species, levels, rows, parts, width)
    mixed = species * levels

    by_core, by_chip = swap_pairs(bands, 0), swap_pairs(bands, 1)
    def flat(value):
        return value.reshape(-1, LANES)

    def in_hbm(*values):
        return [pltpu.with_memory_space_constraint(item, pltpu.HBM) for item in values]

    tracers, winds = flat(species_fractions), flat(cell_flow_ratios)
    sent = pl.pallas_call(
        pack_kernel,
        out_shape=jax.ShapeDtypeStruct((len(tracers) + len(winds), LANES), F32),
        in_specs=[pl.BlockSpec(memory_space=pltpu.HBM)] * 2,
        scratch_shapes=[pltpu.SemaphoreType.DMA((2,))],
        compiler_params=PARAMS,
        name="pack",
    )(*in_hbm(tracers, winds))
    core_band = lax.ppermute(sent, "lat", by_core)
    chip_band = lax.ppermute(sent, "lat", by_chip)

    def arrays(*shapes):
        return [jax.ShapeDtypeStruct(shape, F32) for shape in shapes]

    padded = lons + 2 * PAD
    pairs = all_levels // 2
    operands = (
        layer_pressure_depth.transpose(1, 2, 0),
        layer_thickness_fraction[None],
        cell_kelvin_field.transpose(1, 2, 0),
        daytime_indicator,
        kinetic_factor_times_step[None],
        arrhenius_barrier[None],
        species_yield_matrix.T,
        reagent_pairs,
    )
    early = pl.pallas_call(
        functools.partial(early_kernel, sizes, blocks),
        out_shape=[
            *arrays((rows - 1, 2, lons, mixed)),
            *arrays((2 * rows, lons, mixed), (2 * rows, 2, lons, mixed), (2 * rows, lons, mixed)),
            *arrays((all_levels, pairs, LANES), (reactions, pairs * LANES)),
            jax.ShapeDtypeStruct((substeps, LANES), jnp.int32),
            jax.ShapeDtypeStruct((2 * reactions, 2 * species), jnp.bfloat16),
            jax.ShapeDtypeStruct((species, 2 * reactions), jnp.bfloat16),
        ],
        in_specs=[pl.BlockSpec(memory_space=pltpu.VMEM)] * 2
        + [pl.BlockSpec(memory_space=pltpu.HBM)] * len(operands),
        scratch_shapes=[
            *[pltpu.VMEM(item.shape, item.dtype) for item in operands],
            pltpu.SemaphoreType.DMA((len(operands),)),
            *[pltpu.VMEM((2 * rows, padded, mixed), F32)] * 4,
            *[pltpu.VMEM((pairs, LANES), F32)] * 3,
        ],
        compiler_params=PARAMS,
        cost_estimate=pl.CostEstimate(
            flops=10**7, bytes_accessed=7 * 10**6, transcendentals=10**6
        ),
        name="early",
    )(sent, core_band, *in_hbm(*operands))
    near, prepared = early[:4], early[4:]

    packed = kernel_call(
        functools.partial(advect_kernel, sizes),
        "advect",
        arrays((blocks, rows * width, mixed))[0],
        [(2 * rows, padded, mixed)] * 4
        + [
            (2 * rows, 2, lons, mixed),
            (2 * rows, lons, mixed),
            (2, 2, lons, mixed),
            (2 * rows, padded, mixed),
        ],
    )(*near, chip_band)
    moved = lax.all_to_all(packed, "lev", split_axis=0, concat_axis=0, tiled=True)

    reacted = kernel_call(
        functools.partial(column_kernel, (blocks, levels, species, pairs // 4)),
        "columns",
        arrays(packed.shape)[0],
        [(blocks // 2, mixed, LANES)] * 2,
    )(moved, *prepared)
    returned = lax.all_to_all(reacted, "lev", split_axis=0, concat_axis=0, tiled=True)
    out = kernel_call(
        functools.partial(spread_kernel, sizes),
        "spread",
        arrays((mixed * rows * parts, LANES))[0],
        [],
    )(returned)
    return out.reshape(species_fractions.shape)


def solution(mesh):
    placed = (
        P(None, "lev", "lat", None),
        P(None, "lev", "lat", None),
        P(None, "lat", "lev"),
        P(),
        P(None, "lat", "lev"),
        P(None, "lat", "lev"),
        P(),
        P(),
        P(),
        P(),
    )
    return jax.shard_map(
        body, mesh=mesh, in_specs=placed, out_specs=P(None, "lev", "lat", None), check_vma=False
    )
```

```python
import functools

import jax
import jax.numpy as jnp
from jax import lax
from jax.experimental import pallas as pl
from jax.experimental.pallas import tpu as pltpu
from jax.sharding import PartitionSpec as P

LANES = 128
PAD = 8
SWEEPS = 2
PARAMS = pltpu.CompilerParams(vmem_limit_bytes=16 * 2**20)
F32 = jnp.float32


def limited_slope(left, right):
    return jnp.maximum(jnp.minimum(right, jnp.maximum(left, 0.0)), jnp.minimum(left, 0.0))


def slope_weight(courant):
    return 0.5 * (jnp.abs(courant) - courant * courant)


def face_flux(courant, weight, before, after, before_slope, after_slope):
    ahead = courant > 0.0
    return courant * jnp.where(ahead, before, after) + weight * jnp.where(
        ahead, before_slope, after_slope
    )


def put_cyclic(ref, row, value):
    size = value.shape[0]
    ref[row, PAD : PAD + size] = value
    ref[row, PAD - 1 : PAD] = value[size - 1 :]
    ref[row, PAD + size : PAD + size + 1] = value[:1]


def shifted(ref, row, size, by):
    return ref[row, PAD + by : PAD + by + size]


def lon_step(f_ref, slope_ref, flux_ref, row, courant, weight):
    size = courant.shape[0]
    f, left, right = (shifted(f_ref, row, size, by) for by in (0, -1, 1))
    slope = limited_slope(f - left, right - f)
    put_cyclic(slope_ref, row, slope)
    flux = face_flux(courant, weight, left, f, shifted(slope_ref, row, size, -1), slope)
    put_cyclic(flux_ref, row, flux)
    return f - (shifted(flux_ref, row, size, 1) - flux)


def lat_step(f, weights):
    jumps = [f[i + 1] - f[i] for i in range(len(f) - 1)]
    slopes = [None] + [limited_slope(jumps[i - 1], jumps[i]) for i in range(1, len(f) - 1)]
    fluxes = [
        face_flux(*weights[i - 2], f[i - 1], f[i], slopes[i - 1], slopes[i])
        for i in range(2, len(f) - 1)
    ]
    return [f[i] - (fluxes[i - 1] - fluxes[i - 2]) for i in range(2, len(f) - 2)]


def tracer_rows(sizes, ref, row):
    species, levels, rows, parts, _ = sizes
    return [
        ref[pl.ds(row * parts + k, species * levels, rows * parts), :] for k in range(parts)
    ]


def flow_rows(sizes, ref, which, row, skip=0):
    species, levels, rows, parts, _ = sizes
    found = []
    for k in range(parts):
        start = ((skip + which) * levels * rows + row) * parts + k
        level_rows = ref[pl.ds(start, levels, rows * parts), :]
        tile = jnp.concatenate([level_rows] * (8 // levels), axis=0)
        found.append(jnp.concatenate([tile] * (species * levels // 8), axis=0))
    return found


def turned(tiles):
    return jnp.concatenate([tile.T for tile in tiles], axis=0)


def zonal_weights(flow_ref, row, flow):
    put_cyclic(flow_ref, row, flow)
    courant = 0.5 * (shifted(flow_ref, row, flow.shape[0], -1) + flow)
    return courant, slope_weight(courant)


def near_rows(
    sizes, sent_ref, core_ref, f_out, zonal_out, merid_out, f_ref, slope_ref, flux_ref, flow_ref
):
    rows = sizes[2]
    for side, source in enumerate((sent_ref, core_ref)):
        for row in range(rows):
            at = side * rows + row
            first_sweep(
                sizes, source, row, at, at, f_out, zonal_out, merid_out, f_ref, slope_ref, flux_ref, flow_ref
            )


def first_sweep(
    sizes, source, row, at, to, f_out, zonal_out, merid_out, f_ref, slope_ref, flux_ref, flow_ref, skip=0
):
    species = sizes[0]
    courant, weight = zonal_weights(
        flow_ref, at, turned(flow_rows(sizes, source, 0, row, species))
    )
    zonal_out[to, 0], zonal_out[to, 1] = courant, weight
    merid_out[to] = turned(flow_rows(sizes, source, 1, row, species))
    put_cyclic(f_ref, at, turned(tracer_rows(sizes, source, row)))
    f_out[to, skip : skip + courant.shape[0]] = lon_step(
        f_ref, slope_ref, flux_ref, at, courant, weight
    )


def advect_kernel(
    sizes,
    inner_merid,
    own_ref,
    own_zonal,
    own_merid,
    chip_ref,
    out_ref,
    f_ref,
    slope_ref,
    flux_ref,
    flow_ref,
    halo_zonal,
    halo_merid,
    merid_ref,
    next_ref,
):
    species, levels, rows, parts, width = sizes
    band = lax.axis_index("lat")
    size = own_ref.shape[1]
    chip_at = (band % 2) * rows
    core_at = rows - chip_at
    for row in range(rows):
        first_sweep(
            sizes,
            chip_ref,
            row,
            row,
            chip_at + row,
            f_ref,
            halo_zonal,
            halo_merid,
            next_ref,
            slope_ref,
            flux_ref,
            flow_ref,
            PAD,
        )
        f_ref[core_at + row, PAD : PAD + size] = own_ref[rows + row]
        halo_zonal[core_at + row] = own_zonal[rows + row]
        halo_merid[core_at + row] = own_merid[rows + row]

    def row_of(halo, own, row):
        if 0 <= row < rows:
            return own, row
        return halo, (row + rows if row < 0 else row)

    total = rows * lax.axis_size("lat")
    first_face, last_face = 2 - 2 * SWEEPS, rows + 2 * SWEEPS - 2
    for chunk in range(size // width):
        there = slice(chunk * width, (chunk + 1) * width)
        inner = slice(PAD + chunk * width, PAD + (chunk + 1) * width)

        def merid_at(row):
            ref, at = row_of(halo_merid, own_merid, row)
            return ref[at, there]

        weights = []
        for face in range(first_face, last_face + 1):
            if 1 <= face < rows:
                weights.append((inner_merid[face - 1, 0, there], inner_merid[face - 1, 1, there]))
                continue
            place = band * rows + face
            open_face = jnp.logical_and(place >= 1, place <= total - 1).astype(F32)
            courant = 0.5 * (merid_at(face - 1) + merid_at(face)) * open_face
            weights.append((courant, slope_weight(courant)))
            if face in (0, rows):
                at = face // rows
                merid_ref[at, 0, there], merid_ref[at, 1, there] = weights[-1]
        f = []
        for row in range(-rows, 2 * rows):
            ref, at = row_of(f_ref, own_ref, row)
            f.append(ref[at, there if ref is own_ref else inner])
        for at, value in enumerate(lat_step(f, weights)):
            next_ref[at, inner] = value

    swept = rows + 2 * SWEEPS
    for at in range(swept):
        next_ref[at, PAD - 1 : PAD] = next_ref[at, PAD + size - 1 : PAD + size]
        next_ref[at, PAD + size : PAD + size + 1] = next_ref[at, PAD : PAD + 1]
        ref, there = row_of(halo_zonal, own_zonal, at - 2)
        f_ref[at, PAD : PAD + size] = lon_step(
            next_ref, slope_ref, flux_ref, at, ref[there, 0], ref[there, 1]
        )
    for chunk in range(size // width):
        there = slice(chunk * width, (chunk + 1) * width)
        inner = slice(PAD + chunk * width, PAD + (chunk + 1) * width)
        f = [f_ref[at, inner] for at in range(swept)]
        faces = [(merid_ref, 0), *[(inner_merid, at) for at in range(rows - 1)], (merid_ref, 1)]
        weights = [(ref[at, 0, there], ref[at, 1, there]) for ref, at in faces]
        for row, value in enumerate(lat_step(f, weights)):
            out_ref[chunk, row * width : (row + 1) * width] = value


def spread_kernel(sizes, in_ref, out_ref):
    species, levels, rows, parts, width = sizes
    per_part = LANES // width
    for row in range(rows):
        for k in range(parts):
            found = [
                in_ref[k * per_part + j, row * width : (row + 1) * width] for j in range(per_part)
            ]
            out_ref[pl.ds(row * parts + k, species * levels, rows * parts), :] = jnp.concatenate(
                found, axis=0
            ).T


def paired(groups, ref, place):
    rows, width, all_levels = ref.shape
    by_level = ref[...].reshape(rows * width, all_levels).T
    levels = all_levels // groups
    for pair in range(groups // 2):
        for parity in range(2):
            start = (2 * pair + parity) * levels
            lane = parity * rows * width
            place[pair * levels : (pair + 1) * levels, lane : lane + rows * width] = by_level[
                start : start + levels
            ]


def pack_kernel(tracer_ref, wind_ref, out_ref, sems):
    size = tracer_ref.shape[0]
    copies = [
        pltpu.make_async_copy(tracer_ref, out_ref.at[:size], sems.at[0]),
        pltpu.make_async_copy(wind_ref, out_ref.at[size:], sems.at[1]),
    ]
    for copy in copies:
        copy.start()
    for copy in copies:
        copy.wait()


def early_kernel(sizes, groups, *refs):
    sent_ref, core_ref, inputs, refs = refs[0], refs[1], refs[2:10], refs[10:]
    inner_out, refs = refs[0], refs[1:]
    outputs, refs = refs[:8], refs[8:]
    places, sems = refs[:8], refs[8]
    own_scratch, prepare_scratch = refs[9:13], refs[13:]
    copies = [
        pltpu.make_async_copy(source, place, sems.at[i])
        for i, (source, place) in enumerate(zip(inputs, places, strict=True))
    ]
    for copy in copies:
        copy.start()
    near_rows(sizes, sent_ref, core_ref, *outputs[:3], *own_scratch)
    merid = outputs[2]
    for face in range(1, sizes[2]):
        courant = 0.5 * (merid[face - 1] + merid[face])
        inner_out[face - 1, 0], inner_out[face - 1, 1] = courant, slope_weight(courant)
    for copy in copies:
        copy.wait()
    prepare(groups, *places, *outputs[3:], *prepare_scratch)


def prepare(
    groups,
    depth_ref,
    share_ref,
    kelvin_ref,
    active_ref,
    factor_ref,
    barrier_ref,
    yield_ref,
    pair_ref,
    overlap_out,
    rate_out,
    active_out,
    pick_out,
    yield_out,
    depth_at,
    kelvin_at,
    lower_at,
):
    rows, width, all_levels = depth_ref.shape
    levels = all_levels // groups
    half = LANES // 2
    odd = lax.broadcasted_iota(jnp.int32, (1, LANES), 1) >= half
    species, reactions = yield_ref.shape

    paired(groups, kelvin_ref, kelvin_at)
    paired(groups, depth_ref, depth_at)
    for parity in range(2):
        for row in range(rows):
            lane = (parity * rows + row) * width
            active_out[:, lane : lane + width] = active_ref[:, row, :]

    def column(ref):
        return jnp.broadcast_to(ref[...], (LANES, ref.shape[1])).T

    base = jnp.zeros((1, LANES), F32)
    for pair in range(groups // 2):
        inside = jnp.zeros((1, LANES), F32)
        for level in range(levels):
            at = pair * levels + level
            lower_at[at : at + 1] = inside
            inside = inside + depth_at[at : at + 1]
        other = pltpu.roll(inside, half, 1)
        start = base + jnp.where(odd, other, 0.0)
        here = slice(pair * levels, (pair + 1) * levels)
        lower_at[here] = lower_at[here] + start
        base = base + (inside + other)
    total = base
    lower = lower_at[...]
    upper = lower + depth_at[...]

    share = column(share_ref)
    share_sum = share[0:1]
    for t in range(1, all_levels):
        share_sum = share_sum + share[t : t + 1]
    below = jnp.zeros((1, LANES), F32)
    target_low = below
    for t in range(all_levels):
        below = below + share[t : t + 1]
        target_top = below / share_sum * total
        shared = jnp.maximum(
            jnp.minimum(upper, target_top) - jnp.maximum(lower, target_low), 0.0
        )
        overlap_out[t] = shared / (share[t : t + 1] / share_sum * total)
        target_low = target_top

    factor, barrier = column(factor_ref), column(barrier_ref)
    for at in range(kelvin_at.shape[0]):
        warmth = 300.0 / kelvin_at[at : at + 1] - 1.0
        rate_out[:, at * LANES : (at + 1) * LANES] = factor * jnp.exp(-barrier * warmth)

    one_species = lax.broadcasted_iota(jnp.int32, (2 * species, reactions), 0) % species
    for which in range(2):
        hit = (one_species == pair_ref[which : which + 1, :]).astype(F32)
        pick_out[which * reactions : (which + 1) * reactions] = hit.T.astype(jnp.bfloat16)
    yields = yield_ref[...].astype(F32).astype(jnp.bfloat16)
    yield_out[:, :reactions] = yields
    yield_out[:, reactions:] = yields


def in_two_parts(value):
    high = value.astype(jnp.bfloat16)
    low = (value - high.astype(F32)).astype(jnp.bfloat16)
    return jnp.concatenate([high, low], axis=0)


def column_kernel(
    sizes,
    moved_ref,
    overlap_ref,
    rate_ref,
    active_ref,
    pick_ref,
    yield_ref,
    out_ref,
    source_ref,
    target_ref,
):
    groups, levels, species, tile_pairs = sizes
    half = LANES // 2
    pairs = groups // 2 * levels
    reactions = yield_ref.shape[1] // 2
    odd = lax.broadcasted_iota(jnp.int32, (1, LANES), 1) >= half

    for pair in range(groups // 2):
        both = jnp.concatenate([moved_ref[2 * pair], moved_ref[2 * pair + 1]], axis=0)
        source_ref[pair] = both.T

    def remapped(at):
        pair, level = divmod(at, levels)
        sums = []
        for parity in range(2):
            t = (2 * pair + parity) * levels + level
            acc = None
            for s in range(pairs):
                source = source_ref[s // levels, pl.ds(s % levels, species, levels), :]
                term = overlap_ref[t, s : s + 1, :] * source
                acc = term if acc is None else acc + term
            sums.append(acc)
        kept = jnp.where(odd, sums[1], sums[0])
        crossed = jnp.where(odd, sums[0], sums[1])
        return kept + pltpu.roll(crossed, half, 1)

    tiles = [range(first, first + tile_pairs) for first in range(0, pairs, tile_pairs)]
    q = [jnp.concatenate([remapped(at) for at in tile], axis=1) for tile in tiles]
    for substep in range(active_ref.shape[0]):
        on = jnp.concatenate([active_ref[substep : substep + 1, :]] * tile_pairs, axis=1) > 0
        picked = [
            jnp.dot(pick_ref[...], in_two_parts(value), preferred_element_type=F32) for value in q
        ]
        rates = [
            rate_ref[:, tile[0] * LANES : (tile[-1] + 1) * LANES]
            * found[:reactions]
            * found[reactions:]
            for tile, found in zip(tiles, picked, strict=True)
        ]
        rates = [in_two_parts(value) for value in rates]
        changes = [
            jnp.dot(yield_ref[...], value, preferred_element_type=F32) for value in rates
        ]
        q = [
            jnp.where(on, value + change, value) for value, change in zip(q, changes, strict=True)
        ]
    for tile, value in zip(tiles, q, strict=True):
        for inside, at in enumerate(tile):
            pair, level = divmod(at, levels)
            lane = inside * LANES
            target_ref[pair, pl.ds(level, species, levels), :] = value[:, lane : lane + LANES]

    for pair in range(groups // 2):
        both = target_ref[pair].T
        out_ref[2 * pair], out_ref[2 * pair + 1] = both[:half], both[half:]


def swap_pairs(count, first):
    route = []
    for low in range(first, count - 1, 2):
        route += [(low, low + 1), (low + 1, low)]
    return route


def kernel_call(kernel, name, outs, scratch, cost=None):
    return pl.pallas_call(
        kernel,
        out_shape=outs,
        scratch_shapes=[pltpu.VMEM(shape, F32) for shape in scratch],
        compiler_params=PARAMS,
        cost_estimate=cost,
        name=name,
    )


def body(
    species_fractions,
    cell_flow_ratios,
    layer_pressure_depth,
    layer_thickness_fraction,
    cell_kelvin_field,
    daytime_indicator,
    kinetic_factor_times_step,
    arrhenius_barrier,
    species_yield_matrix,
    reagent_pairs,
):
    species, levels, rows, lons = species_fractions.shape
    all_levels = layer_pressure_depth.shape[0]
    width = layer_pressure_depth.shape[2]
    blocks = lax.axis_size("lev")
    bands = lax.axis_size("lat")
    parts = lons // LANES
    substeps = daytime_indicator.shape[0]
    reactions = kinetic_factor_times_step.shape[0]
    assert 2 * rows * width == LANES and rows == 2 * SWEEPS and blocks % 2 == 0
    sizes = (species, levels, rows, parts, width)
    mixed = species * levels

    by_core, by_chip = swap_pairs(bands, 0), swap_pairs(bands, 1)
    def flat(value):
        return value.reshape(-1, LANES)

    def in_hbm(*values):
        return [pltpu.with_memory_space_constraint(item, pltpu.HBM) for item in values]

    tracers, winds = flat(species_fractions), flat(cell_flow_ratios)
    sent = pl.pallas_call(
        pack_kernel,
        out_shape=jax.ShapeDtypeStruct((len(tracers) + len(winds), LANES), F32),
        in_specs=[pl.BlockSpec(memory_space=pltpu.HBM)] * 2,
        scratch_shapes=[pltpu.SemaphoreType.DMA((2,))],
        compiler_params=PARAMS,
        name="pack",
    )(*in_hbm(tracers, winds))
    core_band = lax.ppermute(sent, "lat", by_core)
    chip_band = lax.ppermute(sent, "lat", by_chip)

    def arrays(*shapes):
        return [jax.ShapeDtypeStruct(shape, F32) for shape in shapes]

    padded = lons + 2 * PAD
    pairs = all_levels // 2
    operands = (
        layer_pressure_depth.transpose(1, 2, 0),
        layer_thickness_fraction[None],
        cell_kelvin_field.transpose(1, 2, 0),
        daytime_indicator,
        kinetic_factor_times_step[None],
        arrhenius_barrier[None],
        species_yield_matrix.T,
        reagent_pairs,
    )
    early = pl.pallas_call(
        functools.partial(early_kernel, sizes, blocks),
        out_shape=[
            *arrays((rows - 1, 2, lons, mixed)),
            *arrays((2 * rows, lons, mixed), (2 * rows, 2, lons, mixed), (2 * rows, lons, mixed)),
            *arrays((all_levels, pairs, LANES), (reactions, pairs * LANES)),
            jax.ShapeDtypeStruct((substeps, LANES), jnp.int32),
            jax.ShapeDtypeStruct((2 * reactions, 2 * species), jnp.bfloat16),
            jax.ShapeDtypeStruct((species, 2 * reactions), jnp.bfloat16),
        ],
        in_specs=[pl.BlockSpec(memory_space=pltpu.VMEM)] * 2
        + [pl.BlockSpec(memory_space=pltpu.HBM)] * len(operands),
        scratch_shapes=[
            *[pltpu.VMEM(item.shape, item.dtype) for item in operands],
            pltpu.SemaphoreType.DMA((len(operands),)),
            *[pltpu.VMEM((2 * rows, padded, mixed), F32)] * 4,
            *[pltpu.VMEM((pairs, LANES), F32)] * 3,
        ],
        compiler_params=PARAMS,
        cost_estimate=pl.CostEstimate(
            flops=10**7, bytes_accessed=7 * 10**6, transcendentals=10**6
        ),
        name="early",
    )(sent, core_band, *in_hbm(*operands))
    near, prepared = early[:4], early[4:]

    packed = kernel_call(
        functools.partial(advect_kernel, sizes),
        "advect",
        arrays((blocks, rows * width, mixed))[0],
        [(2 * rows, padded, mixed)] * 4
        + [
            (2 * rows, 2, lons, mixed),
            (2 * rows, lons, mixed),
            (2, 2, lons, mixed),
            (2 * rows, padded, mixed),
        ],
    )(*near, chip_band)
    moved = lax.all_to_all(packed, "lev", split_axis=0, concat_axis=0, tiled=True)

    reacted = kernel_call(
        functools.partial(column_kernel, (blocks, levels, species, pairs // 4)),
        "columns",
        arrays(packed.shape)[0],
        [(blocks // 2, mixed, LANES)] * 2,
    )(moved, *prepared)
    returned = lax.all_to_all(reacted, "lev", split_axis=0, concat_axis=0, tiled=True)
    out = kernel_call(
        functools.partial(spread_kernel, sizes),
        "spread",
        arrays((mixed * rows * parts, LANES))[0],
        [],
    )(returned)
    return out.reshape(species_fractions.shape)


def solution(mesh):
    placed = (
        P(None, "lev", "lat", None),
        P(None, "lev", "lat", None),
        P(None, "lat", "lev"),
        P(),
        P(None, "lat", "lev"),
        P(None, "lat", "lev"),
        P(),
        P(),
        P(),
        P(),
    )
    return jax.shard_map(
        body, mesh=mesh, in_specs=placed, out_specs=P(None, "lev", "lat", None), check_vma=False
    )
```
